256 devices in a mesh: blk: 8 (over y, x_lo), dp: 32 (over z, x_hi, core).
Axes of the slice: x: 4 (x_hi: 2, x_lo: 2; x = x_hi * 2 + x_lo), y: 4, z: 8, core: 2. Of those that a mesh axis runs over, the one named last changes fastest.
Arguments:
- images: bfloat16 [64, 32, 32, 640], P('dp', None, None, 'blk'), may hold values from -6 to 6
- out_grads: bfloat16 [64, 32, 32, 640], P('dp'), may hold values from -0.046875 to 0.046875
- patch_inverse: bfloat16 [5760, 5760], P('blk', 'dp'), may hold values from -0.5 to 4.5
- output_inverse: bfloat16 [640, 640], replicated, may hold values from -0.5 to 4.5
Outputs:
- preconditioned: float32 [640, 5760], P('dp', 'blk')
The draws below stay inside these ranges and needn't reach their ends.
All inputs are finite; a program needn't handle non-finite values.
Results may differ from the reference program's by a relative error of at most 0.0065.
Values may be sent and summed in bfloat16 or wider, within the bound.
A program may use at most 128 MiB of HBM per device.

```python
import jax
import jax.numpy as jnp
from jax import lax

CIN = 640
COUT = 640
RES = 32
B_DEV = 2
PATCH = 5760
BATCH = 64
N_DP = 32


def symmetric_inverse(key, matrix_order, lowest, highest):
    key_diag, key_normal = jax.random.split(key, 2)
    diagonal = jnp.exp(jax.random.uniform(key_diag, (matrix_order,), jnp.float32, jnp.log(lowest), jnp.log(highest)))
    normal_part = jax.random.normal(key_normal, (matrix_order, matrix_order), jnp.float32)
    blended = normal_part
    coupled = (blended + blended.T) * (0.5 / jnp.sqrt(2.0 * matrix_order))
    return (coupled + jnp.diag(diagonal)).astype(jnp.bfloat16)


def draw_patch_inverse(key, part):
    key = jax.random.fold_in(key, 11)
    return symmetric_inverse(key, PATCH, 1.0, 3.0)


def draw_output_inverse(key, part):
    key = jax.random.fold_in(key, 23)
    return symmetric_inverse(key, COUT, 1.0, 3.0)


def strengthened(drawn, key, source, target, parts, factor):
    def block_of(axis_at):
        return (jnp.arange(drawn.shape[axis_at]) // (drawn.shape[axis_at] // parts)).reshape((-1,) + (1,) * (drawn.ndim - 1 - axis_at))

    first = jax.random.permutation(key, parts)[block_of(target)]
    second = (block_of(target) + parts // 2) % parts
    return jnp.where((block_of(source) == first) | (block_of(source) == second), factor * drawn, drawn)


def shard_levels(stream_key, dims, cuts, least, top_value):
    def one(dim, blocks):
        steps = jax.random.uniform(jax.random.fold_in(jax.random.fold_in(stream_key, 6), dim), (blocks,), jnp.float32, least / len(cuts), top_value / len(cuts))
        return jnp.repeat(jnp.exp(steps), dims[dim] // blocks).reshape((-1,) + (1,) * (len(dims) - dim - 1))

    factor_of = one(*cuts[0])
    for cut in cuts[1:]:
        factor_of = factor_of * one(*cut)
    return factor_of


def noise(own_key, dims, width, bound, pieces=(), held_as=jnp.bfloat16):
    array = jax.random.normal(own_key, dims, jnp.float32) * width
    if len(pieces) > 0:
        array = shard_levels(own_key, dims, pieces, -0.22, 0.18) * array
    return jnp.clip(array, min=-bound, max=bound).astype(held_as)


def bell_draw_with(rng, extent, deviation, most, cuts, heavy, held_as=jnp.bfloat16):
    drawn = deviation * jax.random.normal(rng, extent, jnp.float32)
    if cuts:
        drawn = drawn * shard_levels(rng, extent, cuts, -0.22, 0.18)
    return jnp.clip(strengthened(drawn, jax.random.fold_in(rng, 3), *heavy), -most, most).astype(held_as)


def setup_inputs(seed: int = 0) -> dict:
    keys = jax.random.split(jax.random.key(seed), 5)
    return {
        "images": noise(keys[0], (BATCH, RES, RES, CIN), 1.0, 6.0, ((0, 32), (3, 8))),
        "out_grads": bell_draw_with(keys[1], (BATCH, RES, RES, COUT), (BATCH * RES * RES) ** -0.5, 0.046875, ((0, 32),), (0, 3, 32, 2.75)),
        "patch_inverse": draw_patch_inverse(jax.random.fold_in(keys[4], 71), 0),
        "output_inverse": draw_output_inverse(jax.random.fold_in(keys[4], 71), 0),
    }


def patch_rows(images):
    padded = jnp.pad(images, ((0, 0), (1, 1), (1, 1), (0, 0)))
    height = images.shape[1]
    breadth = images.shape[2]
    shifted = [padded[:, row_tap:row_tap + height, col_tap:col_tap + breadth, :] for row_tap in range(3) for col_tap in range(3)]
    stacked = jnp.stack(shifted, axis=-1)
    return stacked.reshape(-1, images.shape[3] * 9)


def group_gradient(images, out_grads):
    patches = patch_rows(images)
    flat_grads = out_grads.reshape(-1, out_grads.shape[3])
    product = lax.dot_general(flat_grads, patches, (((0,), (0,)), ((), ())), preferred_element_type=jnp.float32)
    return product.astype(jnp.bfloat16)


def reference(images, out_grads, patch_inverse, output_inverse):
    grouped_images = images.reshape(N_DP, B_DEV, RES, RES, CIN)
    grouped_grads = out_grads.reshape(N_DP, B_DEV, RES, RES, COUT)

    def accumulate(summed, members):
        partial_grad = group_gradient(members[0], members[1])
        return summed + partial_grad.astype(jnp.float32), None

    summed, unused = lax.scan(accumulate, jnp.zeros((COUT, PATCH), jnp.float32), (grouped_images, grouped_grads))
    applied = jnp.dot(summed, patch_inverse.astype(jnp.float32).T, precision=lax.Precision.HIGHEST, preferred_element_type=jnp.float32)
    return jnp.dot(output_inverse.astype(jnp.float32).T, applied, precision=lax.Precision.HIGHEST, preferred_element_type=jnp.float32)
```

```python
import functools

import jax
import jax.numpy as jnp
from jax import lax
from jax.experimental import pallas as pl
from jax.experimental.pallas import tpu as pltpu
from jax.sharding import PartitionSpec as P

MESH = pl.DeviceIdType.MESH
BF = jnp.bfloat16
F32 = jnp.float32


def dot(a, b, dims):
    return lax.dot_general(a, b, (dims, ((), ())), preferred_element_type=F32)


def kernel(
    img_h, g_h, p_h, o_h, out_ref,
    img_v, g_v, o_v, pbuf, patches, t_v, sp, dbuf, ssum, rbuf, hbuf, hmat, pcat, acc, pk, pr, fin,
    load_sem, p_send, p_recv, d_send, d_recv, rs_send, rs_recv, ag_send, ag_recv, pl_send, pl_recv, t_send, t_recv,
):
    blk = lax.axis_index("blk")
    dp = lax.axis_index("dp")
    core = dp % 2
    pos = dp // 2
    x_hi = pos % 2
    z = dp // 4
    quarter = core * 2 + x_hi
    sibling = {"blk": blk, "dp": dp + 1 - 2 * core}
    partner = {"blk": blk, "dp": dp + 2 - 4 * x_hi}
    to_blk, to_dp = z, 8 * quarter + blk
    from_blk = dp % 8
    from_quarter = dp // 8
    from_dp = blk * 4 + (from_quarter % 2) * 2 + from_quarter // 2
    stays = jnp.logical_and(to_blk == blk, to_dp == dp)

    loads = [
        pltpu.make_async_copy(img_h, img_v, load_sem.at[0]),
        pltpu.make_async_copy(p_h, pbuf.at[dp % 4], load_sem.at[1]),
        pltpu.make_async_copy(g_h, g_v, load_sem.at[2]),
        pltpu.make_async_copy(o_h, o_v, load_sem.at[3]),
    ]
    for load in loads:
        load.start()

    barrier = pltpu.get_barrier_semaphore()
    pl.semaphore_signal(barrier, inc=1, device_id=sibling, device_id_type=MESH)
    for j in range(1, 16):
        pl.semaphore_signal(
            barrier, inc=1, device_id={"blk": blk, "dp": ((pos + j) % 16) * 2 + core}, device_id_type=MESH
        )
    for j in range(1, 8):
        pl.semaphore_signal(barrier, inc=1, device_id={"blk": (blk + j) % 8, "dp": dp}, device_id_type=MESH)

    @pl.when(jnp.logical_not(stays))
    def _():
        pl.semaphore_signal(barrier, inc=1, device_id={"blk": from_blk, "dp": from_dp}, device_id_type=MESH)

    loads[0].wait()
    eye = (
        lax.broadcasted_iota(jnp.int32, (80, 80), 0) == lax.broadcasted_iota(jnp.int32, (80, 80), 1)
    ).astype(F32).astype(BF)
    img_t = dot(eye, img_v[...], ((1,), (1,)))
    lane = lax.broadcasted_iota(jnp.int32, (80, 2048), 1)
    col = lane & 31
    row = (lane >> 5) & 31
    zero = jnp.zeros((80, 2048), F32)
    for kw in range(3):
        if kw == 0:
            shifted = jnp.where(col == 0, zero, pltpu.roll(img_t, 1, 1))
        elif kw == 1:
            shifted = img_t
        else:
            shifted = jnp.where(col == 31, zero, pltpu.roll(img_t, 2047, 1))
        for kh in range(3):
            if kh == 0:
                piece = jnp.where(row == 0, zero, pltpu.roll(shifted, 32, 1))
            elif kh == 1:
                piece = shifted
            else:
                piece = jnp.where(row == 31, zero, pltpu.roll(shifted, 2016, 1))
            tap = kh * 3 + kw
            patches[80 * tap : 80 * tap + 80, :] = piece.astype(BF)

    pl.semaphore_wait(barrier, 23 + jnp.where(stays, 0, 1))
    loads[1].wait()
    mine = dp % 4
    theirs = (mine + 2) % 4

    def p_copy(slot, index, target):
        return pltpu.make_async_remote_copy(
            src_ref=pbuf.at[slot], dst_ref=pbuf.at[slot], send_sem=p_send.at[index], recv_sem=p_recv.at[index],
            device_id=target, device_id_type=MESH,
        )

    p_out = p_copy(mine, 0, partner)
    p_side = p_copy(mine, 1, sibling)
    p_out.start()
    p_side.start()

    loads[2].wait()
    t_v[0:720, :] = dot(patches[...], g_v[...], ((1,), (0,))).astype(BF)
    t_v[720:768, :] = jnp.zeros((48, 640), BF)
    loads[3].wait()
    for owner in range(2):
        for half in range(2):
            rows = 160 * (2 * owner + half)
            mixed = dot(o_v[rows : rows + 160, :], t_v[...], ((1,), (1,))).astype(BF)
            for k in range(8):
                sp[owner, 2 * k + half, :, 0:768] = mixed[16 * k : 16 * k + 16, :]
            for k in range(6):
                top = 128 + 16 * (k // 3)
                left = 256 * (k % 3)
                sp[owner, 2 * k + half, :, 768:1024] = mixed[top : top + 16, left : left + 256]
            for k in range(6, 8):
                sp[owner, 2 * k + half, :, 768:1024] = jnp.zeros((16, 256), BF)

    d_copy = pltpu.make_async_remote_copy(
        src_ref=sp.at[1 - core], dst_ref=dbuf, send_sem=d_send, recv_sem=d_recv,
        device_id=sibling, device_id_type=MESH,
    )
    d_copy.start()
    p_out.wait_recv()
    p_fwd = p_copy(theirs, 2, sibling)
    p_fwd.start()
    d_copy.wait_recv()
    ssum[...] = (sp[core].astype(F32) + dbuf[...].astype(F32)).astype(BF)

    rs = []
    for j in range(1, 16):
        peer = (pos + j) % 16
        rs.append(
            pltpu.make_async_remote_copy(
                src_ref=ssum.at[peer], dst_ref=rbuf.at[j], send_sem=rs_send.at[j], recv_sem=rs_recv.at[j],
                device_id={"blk": blk, "dp": peer * 2 + core}, device_id_type=MESH,
            )
        )
    for copy in rs:
        copy.start()

    p_side.wait_recv()
    p_fwd.wait_recv()
    prow = lax.broadcasted_iota(jnp.int32, (768, 720), 0)
    pcol = lax.broadcasted_iota(jnp.int32, (768, 720), 1)
    tap = (prow * 52429) >> 22
    wanted = jnp.where(prow < 720, (prow - 80 * tap) * 9 + tap, -1)
    order = (pcol == wanted).astype(F32).astype(BF)
    side_by_side = jnp.concatenate([dot(order, pbuf[s], ((1,), (0,))) for s in range(4)], axis=1)
    pcat[...] = side_by_side.astype(BF)

    for copy in rs:
        copy.wait_recv()
    total = ssum[pos].astype(F32)
    for j in range(1, 16):
        total = total + rbuf[j].astype(F32)
    hbuf[z] = total.astype(BF)

    ag = []
    for j in range(1, 8):
        peer = (z + j) % 8
        ag.append(
            pltpu.make_async_remote_copy(
                src_ref=hbuf.at[z], dst_ref=hbuf.at[z], send_sem=ag_send.at[j], recv_sem=ag_recv.at[j],
                device_id={"blk": blk, "dp": peer * 4 + x_hi * 2 + core}, device_id_type=MESH,
            )
        )
    for copy in ag:
        copy.start()
    for copy in ag:
        copy.wait_recv()
    for k in range(8):
        hmat[16 * k : 16 * k + 16, :] = hbuf[k, :, 0:768]
    for k in range(6):
        top = 128 + 16 * (k // 3)
        left = 256 * (k % 3)
        hmat[top : top + 16, left : left + 256] = hbuf[k, :, 768:1024]
    acc[:, 0:720] = dot(hmat[...], pcat[...], ((1,), (0,)))
    acc[:, 720:768] = jnp.zeros((160, 48), F32)

    for k in range(8):
        pk[k, :, 0:768] = acc[20 * k : 20 * k + 16, :].astype(BF)
        tail = acc[20 * k + 16 : 20 * k + 20, :]
        pieces = [tail[:, 0:256], tail[:, 256:512], tail[:, 512:768], jnp.zeros((4, 256), F32)]
        pk[k, :, 768:1024] = jnp.concatenate(pieces, axis=0).astype(BF)
    plane = []
    for j in range(1, 8):
        peer = (blk + j) % 8
        plane.append(
            pltpu.make_async_remote_copy(
                src_ref=pk.at[peer], dst_ref=pr.at[j], send_sem=pl_send.at[j], recv_sem=pl_recv.at[j],
                device_id={"blk": peer, "dp": dp}, device_id_type=MESH,
            )
        )
    for copy in plane:
        copy.start()
    for copy in plane:
        copy.wait_recv()
    total = pk[blk].astype(F32)
    for j in range(1, 8):
        total = total + pr[j].astype(F32)
    fin[0:16, :] = total[:, 0:720]
    fin[16:20, 0:256] = total[0:4, 768:1024]
    fin[16:20, 256:512] = total[4:8, 768:1024]
    fin[16:20, 512:720] = total[8:12, 768:976]

    def last():
        return pltpu.make_async_remote_copy(
            src_ref=fin, dst_ref=out_ref, send_sem=t_send, recv_sem=t_recv,
            device_id={"blk": to_blk, "dp": to_dp}, device_id_type=MESH,
        )

    @pl.when(stays)
    def _():
        copy = pltpu.make_async_copy(fin, out_ref, t_send)
        copy.start()
        copy.wait()

    @pl.when(jnp.logical_not(stays))
    def _():
        copy = last()
        copy.start()
        copy.wait_recv()
        copy.wait_send()

    p_out.wait_send()
    p_side.wait_send()
    p_fwd.wait_send()
    d_copy.wait_send()
    for copy in rs + ag + plane:
        copy.wait_send()


def on_device(images, out_grads, patch_inverse, output_inverse):
    dma = pltpu.SemaphoreType.DMA
    return pl.pallas_call(
        kernel,
        out_shape=jax.ShapeDtypeStruct((20, 720), F32),
        in_specs=[pl.BlockSpec(memory_space=pl.ANY)] * 4,
        out_specs=pl.BlockSpec(memory_space=pltpu.VMEM),
        scratch_shapes=[
            pltpu.VMEM((2048, 80), BF),
            pltpu.VMEM((2048, 640), BF),
            pltpu.VMEM((640, 640), BF),
            pltpu.VMEM((4, 720, 180), BF),
            pltpu.VMEM((720, 2048), BF),
            pltpu.VMEM((768, 640), BF),
            pltpu.VMEM((2, 16, 16, 1024), BF),
            pltpu.VMEM((16, 16, 1024), BF),
            pltpu.VMEM((16, 16, 1024), BF),
            pltpu.VMEM((16, 16, 1024), BF),
            pltpu.VMEM((8, 16, 1024), BF),
            pltpu.VMEM((160, 768), BF),
            pltpu.VMEM((768, 720), BF),
            pltpu.VMEM((160, 768), F32),
            pltpu.VMEM((8, 16, 1024), BF),
            pltpu.VMEM((8, 16, 1024), BF),
            pltpu.VMEM((20, 720), F32),
            dma((4,)),
            dma((3,)), dma((3,)),
            dma, dma,
            dma((16,)), dma((16,)),
            dma((8,)), dma((8,)),
            dma((8,)), dma((8,)),
            dma, dma,
        ],
        compiler_params=pltpu.CompilerParams(
            collective_id=0, has_side_effects=True, vmem_limit_bytes=48 * 1024 * 1024
        ),
        cost_estimate=pl.CostEstimate(flops=3 * 10**9, bytes_accessed=5 * 10**6, transcendentals=0),
    )(
        images.reshape(2048, 80),
        out_grads.reshape(2048, 640),
        patch_inverse,
        output_inverse,
    )


def solution(mesh):
    placed = (P("dp", None, None, "blk"), P("dp", None, None, None), P("blk", "dp"), P())
    return jax.shard_map(
        on_device, mesh=mesh, in_specs=placed, out_specs=P("dp", "blk"), check_vma=False
    )
```

```python
import functools

import jax
import jax.numpy as jnp
from jax import lax
from jax.experimental import pallas as pl
from jax.experimental.pallas import tpu as pltpu
from jax.sharding import PartitionSpec as P

MESH = pl.DeviceIdType.MESH
BF = jnp.bfloat16
F32 = jnp.float32


def dot(a, b, dims):
    return lax.dot_general(a, b, (dims, ((), ())), preferred_element_type=F32)


def iota(shape, dim):
    return lax.broadcasted_iota(jnp.int32, shape, dim)


def one_hot(hit):
    return jnp.where(hit, 1.0, 0.0).astype(BF)


def kernel(
    img_h, g_h, p_h, o_h, out_ref,
    img_v, g_v, o_v, o_rows, pbuf, patches, t_v,
    sp0, sp1, sp2, db0, db1, db2, ss0, ss1, ss2, rb0, rb1, rb2, hb0, hb1, hb2,
    hmat, pcat, acc, pk, pr,
    load_sem, p_send, p_recv, d_send, d_recv, rs_send, rs_recv, ag_send, ag_recv, f_send, f_recv,
):
    sp, db, ss, rb, hb = (sp0, sp1, sp2), (db0, db1, db2), (ss0, ss1, ss2), (rb0, rb1, rb2), (hb0, hb1, hb2)
    blk = lax.axis_index("blk")
    dp = lax.axis_index("dp")
    core = dp % 2
    pos = dp // 2
    x_hi = pos % 2
    z = dp // 4
    low = dp % 4
    sibling = {"blk": blk, "dp": dp + 1 - 2 * core}
    partner = {"blk": blk, "dp": dp + 2 - 4 * x_hi}
    stays = z == blk

    loads = [
        pltpu.make_async_copy(img_h, img_v, load_sem.at[0]),
        pltpu.make_async_copy(g_h, g_v, load_sem.at[1]),
        pltpu.make_async_copy(o_h, o_v, load_sem.at[2]),
        pltpu.make_async_copy(p_h, pbuf.at[low], load_sem.at[3]),
    ]
    for load in loads:
        load.start()

    barrier = pltpu.get_barrier_semaphore()

    def greet(target):
        pl.semaphore_signal(barrier, inc=1, device_id=target, device_id_type=MESH)

    for j in range(1, 16):
        greet({"blk": blk, "dp": ((pos + j) % 16) * 2 + core})
    for j in range(1, 8):
        greet({"blk": (z + 8 - j) % 8, "dp": blk * 4 + low})

    @pl.when(jnp.logical_not(stays))
    def _():
        greet({"blk": z, "dp": blk * 4 + low})

    greet(sibling)

    loads[0].wait()
    img_t = dot(one_hot(iota((80, 80), 0) == iota((80, 80), 1)), img_v[...], ((1,), (1,)))
    lane = iota((80, 2048), 1)
    col = lane & 31
    row = (lane >> 5) & 31
    zero = jnp.zeros((80, 2048), F32)
    taps = [
        jnp.where(col == 0, zero, pltpu.roll(img_t, 1, 1)),
        img_t,
        jnp.where(col == 31, zero, pltpu.roll(img_t, 2047, 1)),
    ]
    t_v[240:256, :] = jnp.zeros((16, 640), BF)

    loads[2].wait()
    r = iota((640, 640), 0)
    tail = r - 512
    main = r < 512
    r_core = jnp.where(main, r >> 8, tail >> 6)
    r_half = jnp.where(main, (r >> 4) & 1, (tail >> 5) & 1)
    r_own = jnp.where(main, (r >> 5) & 7, (tail >> 2) & 7)
    r_t = jnp.where(main, r & 15, 16 + (tail & 3))
    wanted = 80 * r_own + 40 * r_half + 20 * r_core + r_t
    o_rows[...] = dot(one_hot(iota((640, 640), 1) == wanted), o_v[...], ((1,), (0,))).astype(BF)

    def slab(m, kh):
        for kw in range(3):
            if kh == 0:
                piece = jnp.where(row == 0, zero, pltpu.roll(taps[kw], 32, 1))
            elif kh == 1:
                piece = taps[kw]
            else:
                piece = jnp.where(row == 31, zero, pltpu.roll(taps[kw], 2016, 1))
            patches[80 * kw : 80 * kw + 80, :] = piece.astype(BF)
        t_v[0:240, :] = dot(patches[...], g_v[...], ((1,), (0,))).astype(BF)
        mixed = dot(o_rows[...], t_v[...], ((1,), (1,))).astype(BF)
        sp[m][:, :, :, 0:256] = mixed[0:512].reshape(2, 16, 16, 256)
        for owner in range(2):
            for half in range(2):
                for e in range(2):
                    top = 512 + 64 * owner + 32 * half + 16 * e
                    sp2[owner, 2 * (3 * e + m) + half, :, 256:512] = mixed[top : top + 16]

    def swap(m):
        return pltpu.make_async_remote_copy(
            src_ref=sp[m].at[1 - core], dst_ref=db[m], send_sem=d_send.at[m], recv_sem=d_recv.at[m],
            device_id=sibling, device_id_type=MESH,
        )

    def scatter(m):
        copies = []
        for j in range(1, 16):
            peer = (pos + j) % 16
            copies.append(
                pltpu.make_async_remote_copy(
                    src_ref=ss[m].at[peer], dst_ref=rb[m].at[j],
                    send_sem=rs_send.at[m, j], recv_sem=rs_recv.at[m, j],
                    device_id={"blk": blk, "dp": peer * 2 + core}, device_id_type=MESH,
                )
            )
        return copies

    def gather(m):
        copies = []
        for j in range(1, 8):
            peer = (z + j) % 8
            copies.append(
                pltpu.make_async_remote_copy(
                    src_ref=hb[m].at[z], dst_ref=hb[m].at[z],
                    send_sem=ag_send.at[m, j], recv_sem=ag_recv.at[m, j],
                    device_id={"blk": blk, "dp": peer * 4 + low}, device_id_type=MESH,
                )
            )
        return copies

    def p_copy(slot, index, target):
        return pltpu.make_async_remote_copy(
            src_ref=pbuf.at[slot], dst_ref=pbuf.at[slot], send_sem=p_send.at[index], recv_sem=p_recv.at[index],
            device_id=target, device_id_type=MESH,
        )

    swaps = [swap(m) for m in range(3)]
    scatters = [scatter(m) for m in range(3)]
    gathers = [gather(m) for m in range(3)]

    def pair_sum(m):
        swaps[m].wait_recv()
        ss[m][...] = (sp[m][core].astype(F32) + db[m][...].astype(F32)).astype(BF)
        for copy in scatters[m]:
            copy.start()

    loads[1].wait()
    slab(0, 1)
    for owner in range(2):
        sp2[owner, 12:16, :, 256:512] = jnp.zeros((4, 16, 256), BF)
    pl.semaphore_wait(barrier, 23 + jnp.where(stays, 0, 1))
    swaps[0].start()
    slab(1, 0)
    swaps[1].start()
    pair_sum(0)
    slab(2, 2)
    swaps[2].start()
    pair_sum(1)
    pair_sum(2)

    loads[3].wait()
    theirs = (low + 2) % 4
    p_out = p_copy(low, 0, partner)
    p_side = p_copy(low, 1, sibling)
    p_fwd = p_copy(theirs, 2, sibling)
    p_out.start()
    p_side.start()

    for m in range(3):
        for copy in scatters[m]:
            copy.wait_recv()
        total = ss[m][pos].astype(F32)
        for j in range(1, 16):
            total = total + rb[m][j].astype(F32)
        hb[m][z] = total.astype(BF)
        for copy in gathers[m]:
            copy.start()
        if m == 0:
            p_out.wait_recv()
            p_fwd.start()

    p_side.wait_recv()
    p_fwd.wait_recv()
    c = iota((768, 720), 0)
    part = c >> 8
    within = c & 255
    kw = (within * 52429) >> 22
    kh = jnp.where(part == 0, 1, jnp.where(part == 1, 0, 2))
    source = jnp.where(within < 240, (within - 80 * kw) * 9 + 3 * kh + kw, -1)
    order = one_hot(iota((768, 720), 1) == source)
    stacked = jnp.concatenate([dot(pbuf[s], order, ((1,), (1,))) for s in range(4)], axis=0)
    pcat[0:720, :] = stacked.astype(BF)
    pcat[720:768, :] = jnp.zeros((48, 768), BF)

    for m in range(3):
        for copy in gathers[m]:
            copy.wait_recv()
        for k in range(8):
            hmat[16 * k : 16 * k + 16, 256 * m : 256 * m + 256] = hb[m][k, :, 0:256]
    for m in range(3):
        for e in range(2):
            hmat[128 + 16 * e : 144 + 16 * e, 256 * m : 256 * m + 256] = hb2[3 * e + m, :, 256:512]
    acc[...] = dot(hmat[...], pcat[...], ((1,), (1,)))

    for k in range(8):
        pk[k, :, 0:768] = acc[16 * k : 16 * k + 16, :].astype(BF)
        tail = acc[128 + 4 * k : 132 + 4 * k, :]
        pieces = [tail[:, 0:256], tail[:, 256:512], tail[:, 512:768], jnp.zeros((4, 256), F32)]
        pk[k, :, 768:1024] = jnp.concatenate(pieces, axis=0).astype(BF)
    finals = []
    for j in range(8):
        peer = (blk + j) % 8
        finals.append(
            pltpu.make_async_remote_copy(
                src_ref=pk.at[peer], dst_ref=pr.at[j], send_sem=f_send.at[j], recv_sem=f_recv.at[j],
                device_id={"blk": z, "dp": peer * 4 + low}, device_id_type=MESH,
            )
        )
    for copy in finals[1:]:
        copy.start()

    @pl.when(jnp.logical_not(stays))
    def _():
        finals[0].start()
        finals[0].wait_recv()

    @pl.when(stays)
    def _():
        pr[0] = pk[blk]

    total = pr[0].astype(F32)
    for j in range(1, 8):
        finals[j].wait_recv()
        total = total + pr[j].astype(F32)
    out_ref[0:16, :] = total[:, 0:720]
    out_ref[16:20, 0:256] = total[0:4, 768:1024]
    out_ref[16:20, 256:512] = total[4:8, 768:1024]
    out_ref[16:20, 512:720] = total[8:12, 768:976]

    for copy in swaps + [p_out, p_side, p_fwd] + finals[1:]:
        copy.wait_send()
    for m in range(3):
        for copy in scatters[m] + gathers[m]:
            copy.wait_send()

    @pl.when(jnp.logical_not(stays))
    def _():
        finals[0].wait_send()


def on_device(images, out_grads, patch_inverse, output_inverse):
    dma = pltpu.SemaphoreType.DMA
    return pl.pallas_call(
        kernel,
        out_shape=jax.ShapeDtypeStruct((20, 720), F32),
        in_specs=[pl.BlockSpec(memory_space=pl.ANY)] * 4,
        out_specs=pl.BlockSpec(memory_space=pltpu.VMEM),
        scratch_shapes=[
            pltpu.VMEM((2048, 80), BF),
            pltpu.VMEM((2048, 640), BF),
            pltpu.VMEM((640, 640), BF),
            pltpu.VMEM((640, 640), BF),
            pltpu.VMEM((4, 180, 720), BF),
            pltpu.VMEM((240, 2048), BF),
            pltpu.VMEM((256, 640), BF),
            pltpu.VMEM((2, 16, 16, 256), BF),
            pltpu.VMEM((2, 16, 16, 256), BF),
            pltpu.VMEM((2, 16, 16, 512), BF),
            pltpu.VMEM((16, 16, 256), BF),
            pltpu.VMEM((16, 16, 256), BF),
            pltpu.VMEM((16, 16, 512), BF),
            pltpu.VMEM((16, 16, 256), BF),
            pltpu.VMEM((16, 16, 256), BF),
            pltpu.VMEM((16, 16, 512), BF),
            pltpu.VMEM((16, 16, 256), BF),
            pltpu.VMEM((16, 16, 256), BF),
            pltpu.VMEM((16, 16, 512), BF),
            pltpu.VMEM((8, 16, 256), BF),
            pltpu.VMEM((8, 16, 256), BF),
            pltpu.VMEM((8, 16, 512), BF),
            pltpu.VMEM((160, 768), BF),
            pltpu.VMEM((768, 768), BF),
            pltpu.VMEM((160, 768), F32),
            pltpu.VMEM((8, 16, 1024), BF),
            pltpu.VMEM((8, 16, 1024), BF),
            dma((4,)),
            dma((3,)), dma((3,)),
            dma((3,)), dma((3,)),
            dma((3, 16)), dma((3, 16)),
            dma((3, 8)), dma((3, 8)),
            dma((8,)), dma((8,)),
        ],
        compiler_params=pltpu.CompilerParams(
            collective_id=0, has_side_effects=True, vmem_limit_bytes=60 * 1024 * 1024
        ),
        cost_estimate=pl.CostEstimate(flops=3 * 10**9, bytes_accessed=5 * 10**6, transcendentals=0),
    )(
        images.reshape(2048, 80),
        out_grads.reshape(2048, 640),
        patch_inverse.T,
        output_inverse,
    )


def solution(mesh):
    placed = (P("dp", None, None, "blk"), P("dp", None, None, None), P("blk", "dp"), P())
    return jax.shard_map(
        on_device, mesh=mesh, in_specs=placed, out_specs=P("dp", "blk"), check_vma=False
    )
```

```python
import functools

import jax
import jax.numpy as jnp
from jax import lax
from jax.experimental import pallas as pl
from jax.experimental.pallas import tpu as pltpu
from jax.sharding import PartitionSpec as P

MESH = pl.DeviceIdType.MESH
BF = jnp.bfloat16
F32 = jnp.float32


def dot(a, b, dims):
    return lax.dot_general(a, b, (dims, ((), ())), preferred_element_type=F32)


def iota(shape, dim):
    return lax.broadcasted_iota(jnp.int32, shape, dim)


def one_hot(hit):
    return jnp.where(hit, 1.0, 0.0).astype(BF)


def kernel(
    img_h, g_h, p_h, o_h, out_ref,
    img_v, g_v, o_v, o_rows, pbuf, patches, t_v,
    sp, db, ss, xb, su, rb, hb,
    hmat, pcat, acc, main_out, main_in, tail_out, tail_in,
    load_sem, p_send, p_recv, d_send, d_recv, x_send, x_recv, rs_send, rs_recv, ag_send, ag_recv,
    m_send, m_recv, t_send, t_recv,
):
    blk = lax.axis_index("blk")
    dp = lax.axis_index("dp")
    core = dp % 2
    x_hi = (dp // 2) % 2
    z = dp // 4
    low = dp % 4
    sibling = {"blk": blk, "dp": dp + 1 - 2 * core}
    partner = {"blk": blk, "dp": dp + 2 - 4 * x_hi}
    stays = z == blk

    loads = [
        pltpu.make_async_copy(img_h, img_v, load_sem.at[0]),
        pltpu.make_async_copy(g_h, g_v, load_sem.at[1]),
        pltpu.make_async_copy(o_h, o_v, load_sem.at[2]),
        pltpu.make_async_copy(p_h, pbuf.at[low], load_sem.at[3]),
    ]
    for load in loads:
        load.start()

    barrier = pltpu.get_barrier_semaphore()

    def greet(target):
        pl.semaphore_signal(barrier, inc=1, device_id=target, device_id_type=MESH)

    for j in range(1, 8):
        greet({"blk": (z + 8 - j) % 8, "dp": blk * 4 + low})

    @pl.when(jnp.logical_not(stays))
    def _():
        greet({"blk": z, "dp": blk * 4 + low})

    for j in range(1, 8):
        greet({"blk": blk, "dp": ((z + j) % 8) * 4 + low})
    greet(partner)
    greet(sibling)

    loads[0].wait()
    img_t = dot(one_hot(iota((80, 80), 0) == iota((80, 80), 1)), img_v[...], ((1,), (1,)))
    lane = iota((80, 2048), 1)
    col = lane & 31
    row = (lane >> 5) & 31
    zero = jnp.zeros((80, 2048), F32)
    taps = [
        jnp.where(col == 0, zero, pltpu.roll(img_t, 1, 1)),
        img_t,
        jnp.where(col == 31, zero, pltpu.roll(img_t, 2047, 1)),
    ]
    t_v[240:256, :] = jnp.zeros((16, 640), BF)

    loads[2].wait()
    r = iota((640, 1), 0)
    rest = r - 512
    main = r < 512
    r_core = jnp.where(main, r >> 8, rest >> 6)
    r_half = jnp.where(main, (r >> 7) & 1, (rest >> 5) & 1)
    r_own = jnp.where(main, (r >> 4) & 7, (rest >> 2) & 7)
    r_t = jnp.where(main, r & 15, 16 + (rest & 3))
    wanted = 80 * r_own + 40 * r_half + 20 * r_core + r_t
    o_rows[...] = dot(one_hot(iota((640, 640), 1) == wanted), o_v[...], ((1,), (0,))).astype(BF)

    def slab(m, kh):
        for kw in range(3):
            if kh == 0:
                piece = jnp.where(row == 0, zero, pltpu.roll(taps[kw], 32, 1))
            elif kh == 1:
                piece = taps[kw]
            else:
                piece = jnp.where(row == 31, zero, pltpu.roll(taps[kw], 2016, 1))
            patches[80 * kw : 80 * kw + 80, :] = piece.astype(BF)
        t_v[0:240, :] = dot(patches[...], g_v[...], ((1,), (0,))).astype(BF)
        mixed = dot(o_rows[...], t_v[...], ((1,), (1,))).astype(BF)
        sp[m] = mixed[0:512].reshape(2, 2, 8, 16, 256)
        for owner in range(2):
            for half in range(2):
                for e in range(2):
                    top = 512 + 64 * owner + 32 * half + 16 * e
                    sp[3, owner, half, 3 * e + m] = mixed[top : top + 16]

    def remote(src, dst, send, recv, target):
        return pltpu.make_async_remote_copy(
            src_ref=src, dst_ref=dst, send_sem=send, recv_sem=recv, device_id=target, device_id_type=MESH
        )

    swaps = [remote(sp.at[q, 1 - core], db.at[q], d_send.at[q], d_recv.at[q], sibling) for q in range(4)]
    sides = [remote(ss.at[q, 1 - x_hi], xb.at[q], x_send.at[q], x_recv.at[q], partner) for q in range(4)]
    scatters = [[] for q in range(4)]
    gathers = [[] for q in range(4)]
    for q in range(4):
        for j in (4, 3, 5, 2, 6, 1, 7):
            peer = (z + j) % 8
            target = {"blk": blk, "dp": peer * 4 + low}
            scatters[q].append(
                remote(su.at[q, peer], rb.at[q, j], rs_send.at[q, j], rs_recv.at[q, j], target)
            )
            gathers[q].append(
                remote(hb.at[q, z], hb.at[q, z], ag_send.at[q, j], ag_recv.at[q, j], target)
            )
    theirs = (low + 2) % 4
    p_out = remote(pbuf.at[low], pbuf.at[low], p_send.at[0], p_recv.at[0], partner)
    p_side = remote(pbuf.at[low], pbuf.at[low], p_send.at[1], p_recv.at[1], sibling)
    p_fwd = remote(pbuf.at[theirs], pbuf.at[theirs], p_send.at[2], p_recv.at[2], sibling)
    mains = []
    tails = []
    for j in range(8):
        peer = (blk + j) % 8
        target = {"blk": z, "dp": peer * 4 + low}
        mains.append(remote(main_out.at[peer], main_in.at[j], m_send.at[j], m_recv.at[j], target))
        tails.append(remote(tail_out.at[peer], tail_in.at[j], t_send.at[j], t_recv.at[j], target))

    def pair_sum(q):
        swaps[q].wait_recv()
        ss[q] = (sp[q, core].astype(F32) + db[q].astype(F32)).astype(BF)
        sides[q].start()

    loads[1].wait()
    slab(0, 1)
    pl.semaphore_wait(barrier, 16 + jnp.where(stays, 0, 1))
    swaps[0].start()
    for owner in range(2):
        for half in range(2):
            sp[3, owner, half, 6:8] = jnp.zeros((2, 16, 256), BF)
    slab(1, 0)
    swaps[1].start()
    pair_sum(0)
    slab(2, 2)
    swaps[2].start()
    swaps[3].start()
    pair_sum(1)
    pair_sum(2)
    pair_sum(3)

    loads[3].wait()
    p_out.start()
    p_side.start()

    for q in range(4):
        sides[q].wait_recv()
        su[q] = (ss[q, x_hi].astype(F32) + xb[q].astype(F32)).astype(BF)
        for copy in scatters[q]:
            copy.start()

    for q in range(4):
        total = su[q, z].astype(F32)
        for copy in scatters[q]:
            copy.wait_recv()
        for j in range(1, 8):
            total = total + rb[q, j].astype(F32)
        hb[q, z] = total.astype(BF)
        for copy in gathers[q]:
            copy.start()
        if q == 1:
            p_out.wait_recv()
            p_fwd.start()

    p_side.wait_recv()
    p_fwd.wait_recv()
    c = iota((768, 1), 0)
    part = c >> 8
    within = c & 255
    kw = (within * 52429) >> 22
    kh = jnp.where(part == 0, 1, jnp.where(part == 1, 0, 2))
    source = jnp.where(within < 240, (within - 80 * kw) * 9 + 3 * kh + kw, -1)
    order = one_hot(iota((768, 720), 1) == source)
    stacked = jnp.concatenate([dot(pbuf[s], order, ((1,), (1,))) for s in range(4)], axis=0)
    pcat[0:720, :] = stacked.astype(BF)
    pcat[720:768, :] = jnp.zeros((48, 768), BF)

    for q in range(3):
        for copy in gathers[q]:
            copy.wait_recv()
        hmat[0:128, 256 * q : 256 * q + 256] = hb[q].reshape(128, 256)
    rows = dot(hmat[0:128, :], pcat[...], ((1,), (1,)))

    main_out[...] = rows.astype(BF).reshape(8, 16, 768)
    for copy in mains[1:]:
        copy.start()

    @pl.when(jnp.logical_not(stays))
    def _():
        mains[0].start()

    for copy in gathers[3]:
        copy.wait_recv()
    for m in range(3):
        for e in range(2):
            hmat[128 + 16 * e : 144 + 16 * e, 256 * m : 256 * m + 256] = hb[3, 3 * e + m]
    acc[...] = dot(hmat[128:160, :], pcat[...], ((1,), (1,)))
    for k in range(8):
        tail = acc[4 * k : 4 * k + 4, :]
        pieces = [tail[:, 0:256], tail[:, 256:512], tail[:, 512:768], jnp.zeros((4, 256), F32)]
        tail_out[k] = jnp.concatenate(pieces, axis=0).astype(BF)
    for copy in tails[1:]:
        copy.start()

    @pl.when(jnp.logical_not(stays))
    def _():
        tails[0].start()
        mains[0].wait_recv()

    @pl.when(stays)
    def _():
        main_in[0] = main_out[blk]
        tail_in[0] = tail_out[blk]

    total = main_in[0].astype(F32)
    for j in range(1, 8):
        mains[j].wait_recv()
        total = total + main_in[j].astype(F32)
    out_ref[0:16, :] = total[:, 0:720]

    @pl.when(jnp.logical_not(stays))
    def _():
        tails[0].wait_recv()

    total = tail_in[0].astype(F32)
    for j in range(1, 8):
        tails[j].wait_recv()
        total = total + tail_in[j].astype(F32)
    out_ref[16:20, 0:256] = total[0:4, :]
    out_ref[16:20, 256:512] = total[4:8, :]
    out_ref[16:20, 512:720] = total[8:12, 0:208]

    for copy in swaps + sides + [p_out, p_side, p_fwd] + mains[1:] + tails[1:]:
        copy.wait_send()
    for q in range(4):
        for copy in scatters[q] + gathers[q]:
            copy.wait_send()

    @pl.when(jnp.logical_not(stays))
    def _():
        mains[0].wait_send()
        tails[0].wait_send()


def on_device(images, out_grads, patch_inverse, output_inverse):
    dma = pltpu.SemaphoreType.DMA
    return pl.pallas_call(
        kernel,
        out_shape=jax.ShapeDtypeStruct((20, 720), F32),
        in_specs=[pl.BlockSpec(memory_space=pl.ANY)] * 4,
        out_specs=pl.BlockSpec(memory_space=pltpu.VMEM),
        scratch_shapes=[
            pltpu.VMEM((2048, 80), BF),
            pltpu.VMEM((2048, 640), BF),
            pltpu.VMEM((640, 640), BF),
            pltpu.VMEM((640, 640), BF),
            pltpu.VMEM((4, 180, 720), BF),
            pltpu.VMEM((240, 2048), BF),
            pltpu.VMEM((256, 640), BF),
            pltpu.VMEM((4, 2, 2, 8, 16, 256), BF),
            pltpu.VMEM((4, 2, 8, 16, 256), BF),
            pltpu.VMEM((4, 2, 8, 16, 256), BF),
            pltpu.VMEM((4, 8, 16, 256), BF),
            pltpu.VMEM((4, 8, 16, 256), BF),
            pltpu.VMEM((4, 8, 16, 256), BF),
            pltpu.VMEM((4, 8, 16, 256), BF),
            pltpu.VMEM((160, 768), BF),
            pltpu.VMEM((768, 768), BF),
            pltpu.VMEM((32, 768), F32),
            pltpu.VMEM((8, 16, 768), BF),
            pltpu.VMEM((8, 16, 768), BF),
            pltpu.VMEM((8, 16, 256), BF),
            pltpu.VMEM((8, 16, 256), BF),
            dma((4,)),
            dma((3,)), dma((3,)),
            dma((4,)), dma((4,)),
            dma((4,)), dma((4,)),
            dma((4, 8)), dma((4, 8)),
            dma((4, 8)), dma((4, 8)),
            dma((8,)), dma((8,)),
            dma((8,)), dma((8,)),
        ],
        compiler_params=pltpu.CompilerParams(
            collective_id=0, has_side_effects=True, vmem_limit_bytes=60 * 1024 * 1024
        ),
        cost_estimate=pl.CostEstimate(flops=3 * 10**9, bytes_accessed=5 * 10**6, transcendentals=0),
    )(
        images.reshape(2048, 80),
        out_grads.reshape(2048, 640),
        patch_inverse.T,
        output_inverse,
    )


def solution(mesh):
    placed = (P("dp", None, None, "blk"), P("dp", None, None, None), P("blk", "dp"), P())
    return jax.shard_map(
        on_device, mesh=mesh, in_specs=placed, out_specs=P("dp", "blk"), check_vma=False
    )
```

```python
import functools

import jax
import jax.numpy as jnp
from jax import lax
from jax.experimental import pallas as pl
from jax.experimental.pallas import tpu as pltpu
from jax.sharding import PartitionSpec as P

MESH = pl.DeviceIdType.MESH
BF = jnp.bfloat16
F32 = jnp.float32


def dot(a, b, dims):
    return lax.dot_general(a, b, (dims, ((), ())), preferred_element_type=F32)


def iota(shape, dim):
    return lax.broadcasted_iota(jnp.int32, shape, dim)


def one_hot(hit):
    return jnp.where(hit, 1.0, 0.0).astype(BF)


def kernel(
    img_h, g_h, p_h, o_h, out_ref,
    img_v, g_v, o_v, o_rows, pbuf, patches, t_v,
    sp, db, ss, xb, su, rb, hb,
    hmat, pcat, acc, main_out, main_in, tail_out, tail_in,
    load_sem, p_send, p_recv, d_send, d_recv, x_send, x_recv, rs_send, rs_recv, ag_send, ag_recv,
    m_send, m_recv, t_send, t_recv,
):
    blk = lax.axis_index("blk")
    dp = lax.axis_index("dp")
    core = dp % 2
    x_hi = (dp // 2) % 2
    z = dp // 4
    low = dp % 4
    sibling = {"blk": blk, "dp": dp + 1 - 2 * core}
    partner = {"blk": blk, "dp": dp + 2 - 4 * x_hi}
    stays = z == blk

    loads = [
        pltpu.make_async_copy(img_h, img_v, load_sem.at[0]),
        pltpu.make_async_copy(g_h, g_v, load_sem.at[1]),
        pltpu.make_async_copy(o_h, o_v, load_sem.at[2]),
        pltpu.make_async_copy(p_h, pbuf.at[low], load_sem.at[3]),
    ]
    for load in loads:
        load.start()

    barrier = pltpu.get_barrier_semaphore()

    def greet(target):
        pl.semaphore_signal(barrier, inc=1, device_id=target, device_id_type=MESH)

    for j in range(1, 8):
        greet({"blk": (z + 8 - j) % 8, "dp": blk * 4 + low})

    @pl.when(jnp.logical_not(stays))
    def _():
        greet({"blk": z, "dp": blk * 4 + low})

    for j in range(1, 8):
        greet({"blk": blk, "dp": ((z + j) % 8) * 4 + low})
    greet(partner)
    greet(sibling)

    loads[0].wait()
    img_t = dot(one_hot(iota((80, 80), 0) == iota((80, 80), 1)), img_v[...], ((1,), (1,)))
    lane = iota((80, 2048), 1)
    col = lane & 31
    row = (lane >> 5) & 31
    zero = jnp.zeros((80, 2048), F32)
    taps = [
        jnp.where(col == 0, zero, pltpu.roll(img_t, 1, 1)),
        img_t,
        jnp.where(col == 31, zero, pltpu.roll(img_t, 2047, 1)),
    ]
    t_v[240:256, :] = jnp.zeros((16, 640), BF)

    loads[2].wait()
    r = iota((640, 1), 0)
    rest = r - 512
    main = r < 512
    r_core = jnp.where(main, r >> 8, rest >> 6)
    r_half = jnp.where(main, (r >> 7) & 1, (rest >> 5) & 1)
    r_own = jnp.where(main, (r >> 4) & 7, (rest >> 2) & 7)
    r_t = jnp.where(main, r & 15, 16 + (rest & 3))
    wanted = 80 * ((r_own + 4) & 7) + 40 * r_half + 20 * r_core + r_t
    o_rows[...] = dot(one_hot(iota((640, 640), 1) == wanted), o_v[...], ((1,), (0,))).astype(BF)

    def slab(m, kh, between=None):
        for kw in range(3):
            if kh == 0:
                piece = jnp.where(row == 0, zero, pltpu.roll(taps[kw], 32, 1))
            elif kh == 1:
                piece = taps[kw]
            else:
                piece = jnp.where(row == 31, zero, pltpu.roll(taps[kw], 2016, 1))
            patches[80 * kw : 80 * kw + 80, :] = piece.astype(BF)
        t_v[0:240, :] = dot(patches[...], g_v[...], ((1,), (0,))).astype(BF)
        if between is not None:
            pair_sum(between)
        mixed = dot(o_rows[...], t_v[...], ((1,), (1,))).astype(BF)
        sp[m] = mixed[0:512].reshape(2, 2, 8, 16, 256)
        for owner in range(2):
            for half in range(2):
                for e in range(2):
                    top = 512 + 64 * owner + 32 * half + 16 * e
                    sp[3, owner, half, 3 * e + m] = mixed[top : top + 16]

    def remote(src, dst, send, recv, target):
        return pltpu.make_async_remote_copy(
            src_ref=src, dst_ref=dst, send_sem=send, recv_sem=recv, device_id=target, device_id_type=MESH
        )

    swaps = [remote(sp.at[q, 1 - core], db.at[q], d_send.at[q], d_recv.at[q], sibling) for q in range(4)]
    sides = [
        remote(
            ss.at[q, 1 - x_hi, pl.ds(0, n)], xb.at[q, pl.ds(0, n)], x_send.at[q], x_recv.at[q], partner
        )
        for q, n in enumerate((8, 8, 8, 6))
    ]
    far_first = (4, 3, 5, 2, 6, 1, 7)
    scatters = [[] for q in range(4)]
    gathers = [[] for q in range(4)]
    for q in range(4):
        for j in far_first:
            peer = (z + j) % 8
            target = {"blk": blk, "dp": peer * 4 + low}
            scatters[q].append(
                remote(su.at[q, peer], rb.at[q, j], rs_send.at[q, j], rs_recv.at[q, j], target)
            )
            gathers[q].append(
                remote(hb.at[q, z], hb.at[q, z], ag_send.at[q, j], ag_recv.at[q, j], target)
            )
    theirs = (low + 2) % 4
    p_out = remote(pbuf.at[low], pbuf.at[low], p_send.at[0], p_recv.at[0], partner)
    p_side = remote(pbuf.at[low], pbuf.at[low], p_send.at[1], p_recv.at[1], sibling)
    p_fwd = remote(pbuf.at[theirs], pbuf.at[theirs], p_send.at[2], p_recv.at[2], sibling)
    def pair_sum(q):
        swaps[q].wait_recv()
        ss[q] = (sp[q, core].astype(F32) + db[q].astype(F32)).astype(BF)
        sides[q].start()

    loads[1].wait()
    slab(0, 1)
    pl.semaphore_wait(barrier, 16 + jnp.where(stays, 0, 1))
    swaps[0].start()
    for owner in range(2):
        for half in range(2):
            sp[3, owner, half, 6:8] = jnp.zeros((2, 16, 256), BF)
    xb[3, 6:8] = jnp.zeros((2, 16, 256), BF)
    slab(1, 0)
    swaps[1].start()
    pair_sum(0)
    slab(2, 2, 1)
    swaps[2].start()
    swaps[3].start()
    pair_sum(2)
    pair_sum(3)

    loads[3].wait()
    p_out.start()
    p_side.start()

    for q in range(4):
        sides[q].wait_recv()
        su[q] = (ss[q, x_hi].astype(F32) + xb[q].astype(F32)).astype(BF)
        for copy in scatters[q]:
            copy.start()

    for q in range(4):
        total = su[q, z].astype(F32)
        for copy in scatters[q]:
            copy.wait_recv()
        for j in range(1, 8):
            total = total + rb[q, j].astype(F32)
        hb[q, z] = total.astype(BF)
        for copy in gathers[q]:
            copy.start()
    p_out.wait_recv()
    p_fwd.start()

    p_side.wait_recv()
    p_fwd.wait_recv()
    c = iota((768, 1), 0)
    part = c >> 8
    within = c & 255
    kw = (within * 52429) >> 22
    kh = jnp.where(part == 0, 1, jnp.where(part == 1, 0, 2))
    source = jnp.where(within < 240, (within - 80 * kw) * 9 + 3 * kh + kw, -1)
    order = one_hot(iota((768, 720), 1) == source)
    stacked = jnp.concatenate([dot(pbuf[s], order, ((1,), (1,))) for s in range(4)], axis=0)
    pcat[0:720, :] = stacked.astype(BF)
    pcat[720:768, :] = jnp.zeros((48, 768), BF)

    def to_plane(outgoing, incoming, send, recv, j):
        plane = (z + 12 - j) % 8
        return remote(
            outgoing.at[plane], incoming.at[blk], send.at[j], recv.at[blk], {"blk": z, "dp": plane * 4 + low}
        )

    def from_column(outgoing, incoming, send, recv, b):
        return remote(outgoing.at[b], incoming.at[b], send.at[0], recv.at[b], {"blk": b, "dp": blk * 4 + low})

    mains = [to_plane(main_out, main_in, m_send, m_recv, j) for j in range(8)]
    tails = [to_plane(tail_out, tail_in, t_send, t_recv, j) for j in range(8)]

    def send_rows(group, extra=0):
        for q in range(3):
            for copy, j in zip(gathers[q], far_first):
                if j in group:
                    copy.wait_recv()
        for i, j in enumerate(group):
            for q in range(3):
                hmat[16 * i : 16 * i + 16, 256 * q : 256 * q + 256] = hb[q, (z + 8 - j) % 8]
        n = 16 * len(group)
        product = dot(hmat[0 : n + extra, :], pcat[...], ((1,), (1,)))
        rows = product[0:n].astype(BF)
        for i, j in enumerate(group):
            main_out[(z + 12 - j) % 8] = rows[16 * i : 16 * i + 16, :]
        for j in group:
            if j == 4:
                @pl.when(jnp.logical_not(stays))
                def _():
                    mains[4].start()
            else:
                mains[j].start()
        return product[n:]

    send_rows((0, 1, 7, 2, 6))

    for copy in gathers[3]:
        copy.wait_recv()
    for m in range(3):
        for e in range(2):
            hmat[48 + 16 * e : 64 + 16 * e, 256 * m : 256 * m + 256] = hb[3, 3 * e + m]
    acc[...] = send_rows((3, 5, 4), 32)
    for k in range(8):
        tail = acc[4 * k : 4 * k + 4, :]
        pieces = [tail[:, 0:256], tail[:, 256:512], tail[:, 512:768], jnp.zeros((4, 256), F32)]
        tail_out[(k + 4) % 8] = jnp.concatenate(pieces, axis=0).astype(BF)
    for j in (0, 1, 7, 2, 6, 3, 5):
        tails[j].start()

    @pl.when(jnp.logical_not(stays))
    def _():
        tails[4].start()


    @pl.when(stays)
    def _():
        main_in[blk] = main_out[z]
        tail_in[blk] = tail_out[z]

    def collect(outgoing, incoming, send, recv):
        total = jnp.zeros(incoming.shape[1:], F32)
        for b in range(8):
            @pl.when(jnp.logical_not(jnp.logical_and(stays, blk == b)))
            def _():
                from_column(outgoing, incoming, send, recv, b).wait_recv()

            total = total + incoming[b].astype(F32)
        return total

    total = collect(main_out, main_in, m_send, m_recv)
    out_ref[0:16, :] = total[:, 0:720]
    total = collect(tail_out, tail_in, t_send, t_recv)
    out_ref[16:20, 0:256] = total[0:4, :]
    out_ref[16:20, 256:512] = total[4:8, :]
    out_ref[16:20, 512:720] = total[8:12, 0:208]

    for copy in swaps + sides + [p_out, p_side, p_fwd] + mains[:4] + mains[5:] + tails[:4] + tails[5:]:
        copy.wait_send()
    for q in range(4):
        for copy in scatters[q] + gathers[q]:
            copy.wait_send()

    @pl.when(jnp.logical_not(stays))
    def _():
        mains[4].wait_send()
        tails[4].wait_send()


def on_device(images, out_grads, patch_inverse, output_inverse):
    dma = pltpu.SemaphoreType.DMA
    return pl.pallas_call(
        kernel,
        out_shape=jax.ShapeDtypeStruct((20, 720), F32),
        in_specs=[pl.BlockSpec(memory_space=pl.ANY)] * 4,
        out_specs=pl.BlockSpec(memory_space=pltpu.VMEM),
        scratch_shapes=[
            pltpu.VMEM((2048, 80), BF),
            pltpu.VMEM((2048, 640), BF),
            pltpu.VMEM((640, 640), BF),
            pltpu.VMEM((640, 640), BF),
            pltpu.VMEM((4, 180, 720), BF),
            pltpu.VMEM((240, 2048), BF),
            pltpu.VMEM((256, 640), BF),
            pltpu.VMEM((4, 2, 2, 8, 16, 256), BF),
            pltpu.VMEM((4, 2, 8, 16, 256), BF),
            pltpu.VMEM((4, 2, 8, 16, 256), BF),
            pltpu.VMEM((4, 8, 16, 256), BF),
            pltpu.VMEM((4, 8, 16, 256), BF),
            pltpu.VMEM((4, 8, 16, 256), BF),
            pltpu.VMEM((4, 8, 16, 256), BF),
            pltpu.VMEM((160, 768), BF),
            pltpu.VMEM((768, 768), BF),
            pltpu.VMEM((32, 768), F32),
            pltpu.VMEM((8, 16, 768), BF),
            pltpu.VMEM((8, 16, 768), BF),
            pltpu.VMEM((8, 16, 256), BF),
            pltpu.VMEM((8, 16, 256), BF),
            dma((4,)),
            dma((3,)), dma((3,)),
            dma((4,)), dma((4,)),
            dma((4,)), dma((4,)),
            dma((4, 8)), dma((4, 8)),
            dma((4, 8)), dma((4, 8)),
            dma((8,)), dma((8,)),
            dma((8,)), dma((8,)),
        ],
        compiler_params=pltpu.CompilerParams(
            collective_id=0, has_side_effects=True, vmem_limit_bytes=60 * 1024 * 1024
        ),
        cost_estimate=pl.CostEstimate(flops=3 * 10**9, bytes_accessed=5 * 10**6, transcendentals=0),
    )(
        images.reshape(2048, 80),
        out_grads.reshape(2048, 640),
        patch_inverse.T,
        output_inverse,
    )


def solution(mesh):
    placed = (P("dp", None, None, "blk"), P("dp", None, None, None), P("blk", "dp"), P())
    return jax.shard_map(
        on_device, mesh=mesh, in_specs=placed, out_specs=P("dp", "blk"), check_vma=False
    )
```

```python
import functools

import jax
import jax.numpy as jnp
from jax import lax
from jax.experimental import pallas as pl
from jax.experimental.pallas import tpu as pltpu
from jax.sharding import PartitionSpec as P

MESH = pl.DeviceIdType.MESH
BF = jnp.bfloat16
F32 = jnp.float32
LATE = (2,)
STEPS = (('cross', 2), ('give', 0), ('give', 1), ('give', 2), ('give', 3))


def dot(a, b, dims):
    return lax.dot_general(a, b, (dims, ((), ())), preferred_element_type=F32)


def iota(shape, dim):
    return lax.broadcasted_iota(jnp.int32, shape, dim)


def one_hot(hit):
    return jnp.where(hit, 1.0, 0.0).astype(BF)


def kernel(
    img_h, g_h, p_h, o_h, out_ref,
    img_v, g_v, o_v, o_rows, pbuf, patches, t_v,
    sp, db, ss, xb, su, rb, rz, zf, zb, zx, hb,
    hmat, pcat, acc, main_out, main_in, tail_out, tail_in,
    load_sem, p_send, p_recv, d_send, d_recv, x_send, x_recv, rs_send, rs_recv, ag_send, ag_recv,
    m_send, m_recv, t_send, t_recv,
):
    blk = lax.axis_index("blk")
    dp = lax.axis_index("dp")
    core = dp % 2
    x_hi = (dp // 2) % 2
    z = dp // 4
    low = dp % 4
    sibling = {"blk": blk, "dp": dp + 1 - 2 * core}
    partner = {"blk": blk, "dp": dp + 2 - 4 * x_hi}
    stays = z == blk

    loads = [
        pltpu.make_async_copy(img_h, img_v, load_sem.at[0]),
        pltpu.make_async_copy(g_h, g_v, load_sem.at[1]),
        pltpu.make_async_copy(o_h, o_v, load_sem.at[2]),
        pltpu.make_async_copy(p_h, pbuf.at[low], load_sem.at[3]),
    ]
    for load in loads:
        load.start()

    barrier = pltpu.get_barrier_semaphore()

    def greet(target):
        pl.semaphore_signal(barrier, inc=1, device_id=target, device_id_type=MESH)

    for j in range(1, 8):
        greet({"blk": (z + 8 - j) % 8, "dp": blk * 4 + low})

    @pl.when(jnp.logical_not(stays))
    def _():
        greet({"blk": z, "dp": blk * 4 + low})

    for j in range(1, 8):
        greet({"blk": blk, "dp": ((z + j) % 8) * 4 + low})
    greet(partner)
    greet(sibling)

    loads[0].wait()
    img_t = dot(one_hot(iota((80, 80), 0) == iota((80, 80), 1)), img_v[...], ((1,), (1,)))
    lane = iota((80, 2048), 1)
    col = lane & 31
    row = (lane >> 5) & 31
    zero = jnp.zeros((80, 2048), F32)
    taps = [
        jnp.where(col == 0, zero, pltpu.roll(img_t, 1, 1)),
        img_t,
        jnp.where(col == 31, zero, pltpu.roll(img_t, 2047, 1)),
    ]
    t_v[240:256, :] = jnp.zeros((16, 640), BF)

    loads[2].wait()
    r = iota((640, 1), 0)
    rest = r - 512
    main = r < 512
    r_core = jnp.where(main, r >> 8, rest >> 6)
    r_half = jnp.where(main, (r >> 7) & 1, (rest >> 5) & 1)
    r_own = jnp.where(main, (r >> 4) & 7, (rest >> 2) & 7)
    r_t = jnp.where(main, r & 15, 16 + (rest & 3))
    wanted = 80 * ((r_own + 4) & 7) + 40 * r_half + 20 * r_core + r_t
    o_rows[...] = dot(one_hot(iota((640, 640), 1) == wanted), o_v[...], ((1,), (0,))).astype(BF)

    def slab(m, kh, between=None):
        for kw in range(3):
            if kh == 0:
                piece = jnp.where(row == 0, zero, pltpu.roll(taps[kw], 32, 1))
            elif kh == 1:
                piece = taps[kw]
            else:
                piece = jnp.where(row == 31, zero, pltpu.roll(taps[kw], 2016, 1))
            patches[80 * kw : 80 * kw + 80, :] = piece.astype(BF)
        t_v[0:240, :] = dot(patches[...], g_v[...], ((1,), (0,))).astype(BF)
        if between is not None:
            pair_sum(between)
        mixed = dot(o_rows[...], t_v[...], ((1,), (1,))).astype(BF)
        sp[m] = mixed[0:512].reshape(2, 2, 8, 16, 256)
        for owner in range(2):
            for half in range(2):
                for e in range(2):
                    top = 512 + 64 * owner + 32 * half + 16 * e
                    sp[3, owner, half, 3 * e + m] = mixed[top : top + 16]

    def remote(src, dst, send, recv, target):
        return pltpu.make_async_remote_copy(
            src_ref=src, dst_ref=dst, send_sem=send, recv_sem=recv, device_id=target, device_id_type=MESH
        )

    swaps = [remote(sp.at[q, 1 - core], db.at[q], d_send.at[q], d_recv.at[q], sibling) for q in range(4)]
    sides = {
        q: remote(
            ss.at[q, 1 - x_hi, pl.ds(0, n)], xb.at[q, pl.ds(0, n)], x_send.at[q], x_recv.at[q], partner
        )
        for q, n in enumerate((8, 8, 8, 6))
        if q not in LATE
    }
    late_sides = {
        q: remote(zb.at[i, 1 - x_hi], zx.at[i], x_send.at[q], x_recv.at[q], partner) for i, q in enumerate(LATE)
    }
    far_first = (4, 3, 5, 2, 6, 1, 7)
    scatters = [[] for q in range(4)]
    gathers = [[] for q in range(4)]
    for q in range(4):
        for j in far_first:
            peer = (z + j) % 8
            target = {"blk": blk, "dp": peer * 4 + low}
            source = ss.at[q, :, peer] if q in LATE else su.at[q, peer]
            landing = rz.at[LATE.index(q), j] if q in LATE else rb.at[q, j]
            scatters[q].append(remote(source, landing, rs_send.at[q, j], rs_recv.at[q, j], target))
            gathers[q].append(
                remote(hb.at[q, z], hb.at[q, z], ag_send.at[q, j], ag_recv.at[q, j], target)
            )
    theirs = (low + 2) % 4
    p_out = remote(pbuf.at[low], pbuf.at[low], p_send.at[0], p_recv.at[0], partner)
    p_side = remote(pbuf.at[low], pbuf.at[low], p_send.at[1], p_recv.at[1], sibling)
    p_fwd = remote(pbuf.at[theirs], pbuf.at[theirs], p_send.at[2], p_recv.at[2], sibling)
    def pair_sum(q):
        swaps[q].wait_recv()
        ss[q] = (sp[q, core].astype(F32) + db[q].astype(F32)).astype(BF)
        if q in LATE:
            for copy in scatters[q]:
                copy.start()
        else:
            sides[q].start()

    loads[1].wait()
    slab(0, 1)
    pl.semaphore_wait(barrier, 16 + jnp.where(stays, 0, 1))
    swaps[0].start()
    for owner in range(2):
        for half in range(2):
            sp[3, owner, half, 6:8] = jnp.zeros((2, 16, 256), BF)
    xb[3, 6:8] = jnp.zeros((2, 16, 256), BF)
    slab(1, 0)
    swaps[1].start()
    pair_sum(0)
    slab(2, 2, 1)
    swaps[2].start()
    swaps[3].start()
    pair_sum(2)
    pair_sum(3)

    loads[3].wait()
    p_out.start()
    p_side.start()

    for q in sides:
        sides[q].wait_recv()
        su[q] = (ss[q, x_hi].astype(F32) + xb[q].astype(F32)).astype(BF)
        for copy in scatters[q]:
            copy.start()

    def cross(q):
        i = LATE.index(q)
        for copy in scatters[q]:
            copy.wait_recv()
        total = ss[q, :, z].astype(F32)
        for j in range(1, 8):
            total = total + rz[i, j].astype(F32)
        zf[i] = total
        zb[i] = total.astype(BF)
        late_sides[q].start()

    def give(q):
        if q in LATE:
            late_sides[q].wait_recv()
            total = zf[LATE.index(q), x_hi] + zx[LATE.index(q)].astype(F32)
        else:
            total = su[q, z].astype(F32)
            for copy in scatters[q]:
                copy.wait_recv()
            for j in range(1, 8):
                total = total + rb[q, j].astype(F32)
        hb[q, z] = total.astype(BF)
        for copy in gathers[q]:
            copy.start()

    for act, q in STEPS:
        (cross if act == "cross" else give)(q)

    p_out.wait_recv()
    p_fwd.start()

    p_side.wait_recv()
    p_fwd.wait_recv()
    c = iota((768, 1), 0)
    part = c >> 8
    within = c & 255
    kw = (within * 52429) >> 22
    kh = jnp.where(part == 0, 1, jnp.where(part == 1, 0, 2))
    source = jnp.where(within < 240, (within - 80 * kw) * 9 + 3 * kh + kw, -1)
    order = one_hot(iota((768, 720), 1) == source)
    stacked = jnp.concatenate([dot(pbuf[s], order, ((1,), (1,))) for s in range(4)], axis=0)
    pcat[0:720, :] = stacked.astype(BF)
    pcat[720:768, :] = jnp.zeros((48, 768), BF)

    def to_plane(outgoing, incoming, send, recv, j):
        plane = (z + 12 - j) % 8
        return remote(
            outgoing.at[plane], incoming.at[blk], send.at[j], recv.at[blk], {"blk": z, "dp": plane * 4 + low}
        )

    def from_column(outgoing, incoming, send, recv, b):
        return remote(outgoing.at[b], incoming.at[b], send.at[0], recv.at[b], {"blk": b, "dp": blk * 4 + low})

    mains = [to_plane(main_out, main_in, m_send, m_recv, j) for j in range(8)]
    tails = [to_plane(tail_out, tail_in, t_send, t_recv, j) for j in range(8)]

    def send_rows(group, extra=0):
        for q in range(3):
            for copy, j in zip(gathers[q], far_first):
                if j in group:
                    copy.wait_recv()
        for i, j in enumerate(group):
            for q in range(3):
                hmat[16 * i : 16 * i + 16, 256 * q : 256 * q + 256] = hb[q, (z + 8 - j) % 8]
        n = 16 * len(group)
        product = dot(hmat[0 : n + extra, :], pcat[...], ((1,), (1,)))
        rows = product[0:n].astype(BF)
        for i, j in enumerate(group):
            main_out[(z + 12 - j) % 8] = rows[16 * i : 16 * i + 16, :]
        for j in group:
            if j == 4:
                @pl.when(jnp.logical_not(stays))
                def _():
                    mains[4].start()
            else:
                mains[j].start()
        return product[n:]

    send_rows((0, 1, 7, 2, 6))

    for copy in gathers[3]:
        copy.wait_recv()
    for m in range(3):
        for e in range(2):
            hmat[48 + 16 * e : 64 + 16 * e, 256 * m : 256 * m + 256] = hb[3, 3 * e + m]
    acc[...] = send_rows((3, 5, 4), 32)
    for k in range(8):
        tail = acc[4 * k : 4 * k + 4, :]
        pieces = [tail[:, 0:256], tail[:, 256:512], tail[:, 512:768], jnp.zeros((4, 256), F32)]
        tail_out[(k + 4) % 8] = jnp.concatenate(pieces, axis=0).astype(BF)
    for j in (0, 1, 7, 2, 6, 3, 5):
        tails[j].start()

    @pl.when(jnp.logical_not(stays))
    def _():
        tails[4].start()


    @pl.when(stays)
    def _():
        main_in[blk] = main_out[z]
        tail_in[blk] = tail_out[z]

    def collect(outgoing, incoming, send, recv):
        total = jnp.zeros(incoming.shape[1:], F32)
        for b in range(8):
            @pl.when(jnp.logical_not(jnp.logical_and(stays, blk == b)))
            def _():
                from_column(outgoing, incoming, send, recv, b).wait_recv()

            total = total + incoming[b].astype(F32)
        return total

    total = collect(main_out, main_in, m_send, m_recv)
    out_ref[0:16, :] = total[:, 0:720]
    total = collect(tail_out, tail_in, t_send, t_recv)
    out_ref[16:20, 0:256] = total[0:4, :]
    out_ref[16:20, 256:512] = total[4:8, :]
    out_ref[16:20, 512:720] = total[8:12, 0:208]

    for copy in swaps + list(sides.values()) + list(late_sides.values()) + [p_out, p_side, p_fwd] + mains[:4] + mains[5:] + tails[:4] + tails[5:]:
        copy.wait_send()
    for q in range(4):
        for copy in scatters[q] + gathers[q]:
            copy.wait_send()

    @pl.when(jnp.logical_not(stays))
    def _():
        mains[4].wait_send()
        tails[4].wait_send()


def on_device(images, out_grads, patch_inverse, output_inverse):
    dma = pltpu.SemaphoreType.DMA
    return pl.pallas_call(
        kernel,
        out_shape=jax.ShapeDtypeStruct((20, 720), F32),
        in_specs=[pl.BlockSpec(memory_space=pl.ANY)] * 4,
        out_specs=pl.BlockSpec(memory_space=pltpu.VMEM),
        scratch_shapes=[
            pltpu.VMEM((2048, 80), BF),
            pltpu.VMEM((2048, 640), BF),
            pltpu.VMEM((640, 640), BF),
            pltpu.VMEM((640, 640), BF),
            pltpu.VMEM((4, 180, 720), BF),
            pltpu.VMEM((240, 2048), BF),
            pltpu.VMEM((256, 640), BF),
            pltpu.VMEM((4, 2, 2, 8, 16, 256), BF),
            pltpu.VMEM((4, 2, 8, 16, 256), BF),
            pltpu.VMEM((4, 2, 8, 16, 256), BF),
            pltpu.VMEM((4, 8, 16, 256), BF),
            pltpu.VMEM((4, 8, 16, 256), BF),
            pltpu.VMEM((4, 8, 16, 256), BF),
            pltpu.VMEM((len(LATE), 8, 2, 16, 256), BF),
            pltpu.VMEM((len(LATE), 2, 16, 256), F32),
            pltpu.VMEM((len(LATE), 2, 16, 256), BF),
            pltpu.VMEM((len(LATE), 16, 256), BF),
            pltpu.VMEM((4, 8, 16, 256), BF),
            pltpu.VMEM((160, 768), BF),
            pltpu.VMEM((768, 768), BF),
            pltpu.VMEM((32, 768), F32),
            pltpu.VMEM((8, 16, 768), BF),
            pltpu.VMEM((8, 16, 768), BF),
            pltpu.VMEM((8, 16, 256), BF),
            pltpu.VMEM((8, 16, 256), BF),
            dma((4,)),
            dma((3,)), dma((3,)),
            dma((4,)), dma((4,)),
            dma((4,)), dma((4,)),
            dma((4, 8)), dma((4, 8)),
            dma((4, 8)), dma((4, 8)),
            dma((8,)), dma((8,)),
            dma((8,)), dma((8,)),
        ],
        compiler_params=pltpu.CompilerParams(
            collective_id=0, has_side_effects=True, vmem_limit_bytes=60 * 1024 * 1024
        ),
        cost_estimate=pl.CostEstimate(flops=3 * 10**9, bytes_accessed=5 * 10**6, transcendentals=0),
    )(
        images.reshape(2048, 80),
        out_grads.reshape(2048, 640),
        patch_inverse.T,
        output_inverse,
    )


def solution(mesh):
    placed = (P("dp", None, None, "blk"), P("dp", None, None, None), P("blk", "dp"), P())
    return jax.shard_map(
        on_device, mesh=mesh, in_specs=placed, out_specs=P("dp", "blk"), check_vma=False
    )
```

```python
import functools

import jax
import jax.numpy as jnp
from jax import lax
from jax.experimental import pallas as pl
from jax.experimental.pallas import tpu as pltpu
from jax.sharding import PartitionSpec as P

MESH = pl.DeviceIdType.MESH
BF = jnp.bfloat16
F32 = jnp.float32
LATE = (2,)
STEPS = (('cross', 2), ('give', 0), ('give', 1), ('give', 2), ('give', 3))


def dot(a, b, dims):
    return lax.dot_general(a, b, (dims, ((), ())), preferred_element_type=F32)


def iota(shape, dim):
    return lax.broadcasted_iota(jnp.int32, shape, dim)


def one_hot(hit):
    return jnp.where(hit, 1.0, 0.0).astype(BF)


def kernel(
    img_h, g_h, p_h, o_h, out_ref,
    img_v, g_v, o_v, o_rows, pbuf, patches, t_v,
    own, sp, db, ss, xb, su, rb, rz, zf, zb, zx, hb,
    hmat, pcat, acc, main_out, main_in, tail_out, tail_in,
    load_sem, p_send, p_recv, d_send, d_recv, x_send, x_recv, rs_send, rs_recv, ag_send, ag_recv,
    m_send, m_recv, t_send, t_recv,
):
    blk = lax.axis_index("blk")
    dp = lax.axis_index("dp")
    core = dp % 2
    x_hi = (dp // 2) % 2
    z = dp // 4
    low = dp % 4
    sibling = {"blk": blk, "dp": dp + 1 - 2 * core}
    partner = {"blk": blk, "dp": dp + 2 - 4 * x_hi}
    stays = z == blk

    loads = [
        pltpu.make_async_copy(img_h, img_v, load_sem.at[0]),
        pltpu.make_async_copy(g_h, g_v, load_sem.at[1]),
        pltpu.make_async_copy(o_h, o_v, load_sem.at[2]),
        pltpu.make_async_copy(p_h, pbuf.at[low], load_sem.at[3]),
    ]
    for load in loads:
        load.start()

    barrier = pltpu.get_barrier_semaphore()

    def greet(target):
        pl.semaphore_signal(barrier, inc=1, device_id=target, device_id_type=MESH)

    for j in range(1, 8):
        greet({"blk": (z + 8 - j) % 8, "dp": blk * 4 + low})

    @pl.when(jnp.logical_not(stays))
    def _():
        greet({"blk": z, "dp": blk * 4 + low})

    for j in range(1, 8):
        greet({"blk": blk, "dp": ((z + j) % 8) * 4 + low})
    greet(partner)
    greet(sibling)

    loads[0].wait()
    img_t = dot(one_hot(iota((80, 80), 0) == iota((80, 80), 1)), img_v[...], ((1,), (1,)))
    lane = iota((80, 2048), 1)
    col = lane & 31
    row = (lane >> 5) & 31
    zero = jnp.zeros((80, 2048), F32)
    taps = [
        jnp.where(col == 0, zero, pltpu.roll(img_t, 1, 1)),
        img_t,
        jnp.where(col == 31, zero, pltpu.roll(img_t, 2047, 1)),
    ]
    t_v[240:256, :] = jnp.zeros((16, 640), BF)

    loads[2].wait()
    r = iota((640, 1), 0)
    r_core = jnp.where(r < 320, 0, 1)
    r = r - 320 * r_core
    rest = r - 256
    main = r < 256
    r_half = jnp.where(main, r >> 7, rest >> 5)
    r_own = jnp.where(main, (r >> 4) & 7, (rest >> 2) & 7)
    r_t = jnp.where(main, r & 15, 16 + (rest & 3))
    wanted = 80 * ((r_own + 4) & 7) + 40 * r_half + 20 * r_core + r_t
    ordered = dot(one_hot(iota((640, 640), 1) == wanted), o_v[...], ((1,), (0,))).astype(BF)
    o_rows[...] = ordered.reshape(2, 320, 640)

    def slab(kh):
        for kw in range(3):
            if kh == 0:
                piece = jnp.where(row == 0, zero, pltpu.roll(taps[kw], 32, 1))
            elif kh == 1:
                piece = taps[kw]
            else:
                piece = jnp.where(row == 31, zero, pltpu.roll(taps[kw], 2016, 1))
            patches[80 * kw : 80 * kw + 80, :] = piece.astype(BF)
        t_v[0:240, :] = dot(patches[...], g_v[...], ((1,), (0,))).astype(BF)

    def mix(m, side, target):
        mixed = dot(o_rows[side], t_v[...], ((1,), (1,))).astype(target.dtype)
        target[m] = mixed[0:256].reshape(2, 8, 16, 256)
        for half in range(2):
            for e in range(2):
                top = 256 + 32 * half + 16 * e
                target[3, half, 3 * e + m] = mixed[top : top + 16]

    def remote(src, dst, send, recv, target):
        return pltpu.make_async_remote_copy(
            src_ref=src, dst_ref=dst, send_sem=send, recv_sem=recv, device_id=target, device_id_type=MESH
        )

    swaps = [remote(sp.at[q], db.at[q], d_send.at[q], d_recv.at[q], sibling) for q in range(4)]
    sides = {
        q: remote(
            ss.at[q, 1 - x_hi, pl.ds(0, n)], xb.at[q, pl.ds(0, n)], x_send.at[q], x_recv.at[q], partner
        )
        for q, n in enumerate((8, 8, 8, 6))
        if q not in LATE
    }
    late_sides = {
        q: remote(zb.at[i, 1 - x_hi], zx.at[i], x_send.at[q], x_recv.at[q], partner) for i, q in enumerate(LATE)
    }
    far_first = (4, 3, 5, 2, 6, 1, 7)
    scatters = [[] for q in range(4)]
    gathers = [[] for q in range(4)]
    for q in range(4):
        for j in far_first:
            peer = (z + j) % 8
            target = {"blk": blk, "dp": peer * 4 + low}
            source = ss.at[q, :, peer] if q in LATE else su.at[q, peer]
            landing = rz.at[LATE.index(q), j] if q in LATE else rb.at[q, j]
            scatters[q].append(remote(source, landing, rs_send.at[q, j], rs_recv.at[q, j], target))
            gathers[q].append(
                remote(hb.at[q, z], hb.at[q, z], ag_send.at[q, j], ag_recv.at[q, j], target)
            )
    theirs = (low + 2) % 4
    p_out = remote(pbuf.at[low], pbuf.at[low], p_send.at[0], p_recv.at[0], partner)
    p_side = remote(pbuf.at[low], pbuf.at[low], p_send.at[1], p_recv.at[1], sibling)
    p_fwd = remote(pbuf.at[theirs], pbuf.at[theirs], p_send.at[2], p_recv.at[2], sibling)
    def pair_sum(q):
        swaps[q].wait_recv()
        ss[q] = (own[q] + db[q].astype(F32)).astype(BF)
        if q in LATE:
            for copy in scatters[q]:
                copy.start()
        else:
            sides[q].start()

    loads[1].wait()
    slab(1)
    mix(0, 1 - core, sp)
    pl.semaphore_wait(barrier, 16 + jnp.where(stays, 0, 1))
    swaps[0].start()
    mix(0, core, own)
    for half in range(2):
        sp[3, half, 6:8] = jnp.zeros((2, 16, 256), BF)
        own[3, half, 6:8] = jnp.zeros((2, 16, 256), F32)
    xb[3, 6:8] = jnp.zeros((2, 16, 256), BF)
    slab(0)
    mix(1, 1 - core, sp)
    swaps[1].start()
    pair_sum(0)
    mix(1, core, own)
    slab(2)
    pair_sum(1)
    mix(2, 1 - core, sp)
    swaps[2].start()
    swaps[3].start()
    mix(2, core, own)
    pair_sum(2)
    pair_sum(3)

    loads[3].wait()
    p_out.start()
    p_side.start()

    for q in sides:
        sides[q].wait_recv()
        su[q] = (ss[q, x_hi].astype(F32) + xb[q].astype(F32)).astype(BF)
        for copy in scatters[q]:
            copy.start()

    def cross(q):
        i = LATE.index(q)
        for copy in scatters[q]:
            copy.wait_recv()
        total = ss[q, :, z].astype(F32)
        for j in range(1, 8):
            total = total + rz[i, j].astype(F32)
        zf[i] = total
        zb[i] = total.astype(BF)
        late_sides[q].start()

    def give(q):
        if q in LATE:
            late_sides[q].wait_recv()
            total = zf[LATE.index(q), x_hi] + zx[LATE.index(q)].astype(F32)
        else:
            total = su[q, z].astype(F32)
            for copy in scatters[q]:
                copy.wait_recv()
            for j in range(1, 8):
                total = total + rb[q, j].astype(F32)
        hb[q, z] = total.astype(BF)
        for copy in gathers[q]:
            copy.start()

    for act, q in STEPS:
        (cross if act == "cross" else give)(q)

    p_out.wait_recv()
    p_fwd.start()

    p_side.wait_recv()
    p_fwd.wait_recv()
    c = iota((768, 1), 0)
    part = c >> 8
    within = c & 255
    kw = (within * 52429) >> 22
    kh = jnp.where(part == 0, 1, jnp.where(part == 1, 0, 2))
    source = jnp.where(within < 240, (within - 80 * kw) * 9 + 3 * kh + kw, -1)
    order = one_hot(iota((768, 720), 1) == source)
    stacked = jnp.concatenate([dot(pbuf[s], order, ((1,), (1,))) for s in range(4)], axis=0)
    pcat[0:720, :] = stacked.astype(BF)
    pcat[720:768, :] = jnp.zeros((48, 768), BF)

    def to_plane(outgoing, incoming, send, recv, j):
        plane = (z + 12 - j) % 8
        return remote(
            outgoing.at[plane], incoming.at[blk], send.at[j], recv.at[blk], {"blk": z, "dp": plane * 4 + low}
        )

    def from_column(outgoing, incoming, send, recv, b):
        return remote(outgoing.at[b], incoming.at[b], send.at[0], recv.at[b], {"blk": b, "dp": blk * 4 + low})

    mains = [to_plane(main_out, main_in, m_send, m_recv, j) for j in range(8)]
    tails = [to_plane(tail_out, tail_in, t_send, t_recv, j) for j in range(8)]

    def send_rows(group, extra=0):
        for q in range(3):
            for copy, j in zip(gathers[q], far_first):
                if j in group:
                    copy.wait_recv()
        for i, j in enumerate(group):
            for q in range(3):
                hmat[16 * i : 16 * i + 16, 256 * q : 256 * q + 256] = hb[q, (z + 8 - j) % 8]
        n = 16 * len(group)
        product = dot(hmat[0 : n + extra, :], pcat[...], ((1,), (1,)))
        rows = product[0:n].astype(BF)
        for i, j in enumerate(group):
            main_out[(z + 12 - j) % 8] = rows[16 * i : 16 * i + 16, :]
        for j in group:
            if j == 4:
                @pl.when(jnp.logical_not(stays))
                def _():
                    mains[4].start()
            else:
                mains[j].start()
        return product[n:]

    send_rows((0, 1, 7, 2, 6))

    for copy in gathers[3]:
        copy.wait_recv()
    for m in range(3):
        for e in range(2):
            hmat[48 + 16 * e : 64 + 16 * e, 256 * m : 256 * m + 256] = hb[3, 3 * e + m]
    acc[...] = send_rows((3, 5, 4), 32)
    for k in range(8):
        tail = acc[4 * k : 4 * k + 4, :]
        pieces = [tail[:, 0:256], tail[:, 256:512], tail[:, 512:768], jnp.zeros((4, 256), F32)]
        tail_out[(k + 4) % 8] = jnp.concatenate(pieces, axis=0).astype(BF)
    for j in (0, 1, 7, 2, 6, 3, 5):
        tails[j].start()

    @pl.when(jnp.logical_not(stays))
    def _():
        tails[4].start()


    @pl.when(stays)
    def _():
        main_in[blk] = main_out[z]
        tail_in[blk] = tail_out[z]

    def collect(outgoing, incoming, send, recv):
        total = jnp.zeros(incoming.shape[1:], F32)
        for b in range(8):
            @pl.when(jnp.logical_not(jnp.logical_and(stays, blk == b)))
            def _():
                from_column(outgoing, incoming, send, recv, b).wait_recv()

            total = total + incoming[b].astype(F32)
        return total

    total = collect(main_out, main_in, m_send, m_recv)
    out_ref[0:16, :] = total[:, 0:720]
    total = collect(tail_out, tail_in, t_send, t_recv)
    out_ref[16:20, 0:256] = total[0:4, :]
    out_ref[16:20, 256:512] = total[4:8, :]
    out_ref[16:20, 512:720] = total[8:12, 0:208]

    for copy in swaps + list(sides.values()) + list(late_sides.values()) + [p_out, p_side, p_fwd] + mains[:4] + mains[5:] + tails[:4] + tails[5:]:
        copy.wait_send()
    for q in range(4):
        for copy in scatters[q] + gathers[q]:
            copy.wait_send()

    @pl.when(jnp.logical_not(stays))
    def _():
        mains[4].wait_send()
        tails[4].wait_send()


def on_device(images, out_grads, patch_inverse, output_inverse):
    dma = pltpu.SemaphoreType.DMA
    return pl.pallas_call(
        kernel,
        out_shape=jax.ShapeDtypeStruct((20, 720), F32),
        in_specs=[pl.BlockSpec(memory_space=pl.ANY)] * 4,
        out_specs=pl.BlockSpec(memory_space=pltpu.VMEM),
        scratch_shapes=[
            pltpu.VMEM((2048, 80), BF),
            pltpu.VMEM((2048, 640), BF),
            pltpu.VMEM((640, 640), BF),
            pltpu.VMEM((2, 320, 640), BF),
            pltpu.VMEM((4, 180, 720), BF),
            pltpu.VMEM((240, 2048), BF),
            pltpu.VMEM((256, 640), BF),
            pltpu.VMEM((4, 2, 8, 16, 256), F32),
            pltpu.VMEM((4, 2, 8, 16, 256), BF),
            pltpu.VMEM((4, 2, 8, 16, 256), BF),
            pltpu.VMEM((4, 2, 8, 16, 256), BF),
            pltpu.VMEM((4, 8, 16, 256), BF),
            pltpu.VMEM((4, 8, 16, 256), BF),
            pltpu.VMEM((4, 8, 16, 256), BF),
            pltpu.VMEM((len(LATE), 8, 2, 16, 256), BF),
            pltpu.VMEM((len(LATE), 2, 16, 256), F32),
            pltpu.VMEM((len(LATE), 2, 16, 256), BF),
            pltpu.VMEM((len(LATE), 16, 256), BF),
            pltpu.VMEM((4, 8, 16, 256), BF),
            pltpu.VMEM((160, 768), BF),
            pltpu.VMEM((768, 768), BF),
            pltpu.VMEM((32, 768), F32),
            pltpu.VMEM((8, 16, 768), BF),
            pltpu.VMEM((8, 16, 768), BF),
            pltpu.VMEM((8, 16, 256), BF),
            pltpu.VMEM((8, 16, 256), BF),
            dma((4,)),
            dma((3,)), dma((3,)),
            dma((4,)), dma((4,)),
            dma((4,)), dma((4,)),
            dma((4, 8)), dma((4, 8)),
            dma((4, 8)), dma((4, 8)),
            dma((8,)), dma((8,)),
            dma((8,)), dma((8,)),
        ],
        compiler_params=pltpu.CompilerParams(
            collective_id=0, has_side_effects=True, vmem_limit_bytes=60 * 1024 * 1024
        ),
        cost_estimate=pl.CostEstimate(flops=3 * 10**9, bytes_accessed=5 * 10**6, transcendentals=0),
    )(
        images.reshape(2048, 80),
        out_grads.reshape(2048, 640),
        patch_inverse.T,
        output_inverse,
    )


def solution(mesh):
    placed = (P("dp", None, None, "blk"), P("dp", None, None, None), P("blk", "dp"), P())
    return jax.shard_map(
        on_device, mesh=mesh, in_specs=placed, out_specs=P("dp", "blk"), check_vma=False
    )
```

```python
import functools

import jax
import jax.numpy as jnp
from jax import lax
from jax.experimental import pallas as pl
from jax.experimental.pallas import tpu as pltpu
from jax.sharding import PartitionSpec as P

MESH = pl.DeviceIdType.MESH
BF = jnp.bfloat16
F32 = jnp.float32
LATE = (2,)
STEPS = (('cross', 2), ('give', 0), ('give', 1), ('give', 2), ('give', 3))


def dot(a, b, dims):
    return lax.dot_general(a, b, (dims, ((), ())), preferred_element_type=F32)


def iota(shape, dim):
    return lax.broadcasted_iota(jnp.int32, shape, dim)


def one_hot(hit):
    return jnp.where(hit, 1.0, 0.0).astype(BF)


def kernel(
    img_h, g_h, p_h, o_h, out_ref,
    img_v, g_v, o_v, o_rows, pbuf, patches, t_v,
    own, sp, db, ss, xb, su, rb, rz, zf, zb, zx, hb,
    hmat, pcat, acc, main_out, main_in, tail_out, tail_in,
    load_sem, p_send, p_recv, d_send, d_recv, x_send, x_recv, rs_send, rs_recv, ag_send, ag_recv,
    m_send, m_recv, t_send, t_recv,
):
    blk = lax.axis_index("blk")
    dp = lax.axis_index("dp")
    core = dp % 2
    x_hi = (dp // 2) % 2
    z = dp // 4
    low = dp % 4
    sibling = {"blk": blk, "dp": dp + 1 - 2 * core}
    partner = {"blk": blk, "dp": dp + 2 - 4 * x_hi}
    stays = z == blk

    loads = [
        pltpu.make_async_copy(img_h, img_v, load_sem.at[0]),
        pltpu.make_async_copy(g_h.at[0:1024], g_v.at[0:1024], load_sem.at[1]),
        pltpu.make_async_copy(o_h, o_v, load_sem.at[2]),
        pltpu.make_async_copy(p_h, pbuf.at[low], load_sem.at[3]),
        pltpu.make_async_copy(g_h.at[1024:2048], g_v.at[1024:2048], load_sem.at[4]),
    ]
    for n in (0, 2, 1, 4, 3):
        loads[n].start()

    barrier = pltpu.get_barrier_semaphore()

    def greet(target):
        pl.semaphore_signal(barrier, inc=1, device_id=target, device_id_type=MESH)

    for j in range(1, 8):
        greet({"blk": (z + 8 - j) % 8, "dp": blk * 4 + low})

    @pl.when(jnp.logical_not(stays))
    def _():
        greet({"blk": z, "dp": blk * 4 + low})

    for j in range(1, 8):
        greet({"blk": blk, "dp": ((z + j) % 8) * 4 + low})
    greet(partner)
    greet(sibling)

    loads[0].wait()
    img_t = dot(one_hot(iota((80, 80), 0) == iota((80, 80), 1)), img_v[...], ((1,), (1,)))
    lane = iota((80, 2048), 1)
    col = lane & 31
    row = (lane >> 5) & 31
    zero = jnp.zeros((80, 2048), F32)
    taps = [
        jnp.where(col == 0, zero, pltpu.roll(img_t, 1, 1)),
        img_t,
        jnp.where(col == 31, zero, pltpu.roll(img_t, 2047, 1)),
    ]
    t_v[240:256, :] = jnp.zeros((16, 640), BF)

    loads[2].wait()
    r = iota((640, 1), 0)
    r_core = jnp.where(r < 320, 0, 1)
    r = r - 320 * r_core
    rest = r - 256
    main = r < 256
    r_half = jnp.where(main, r >> 7, rest >> 5)
    r_own = jnp.where(main, (r >> 4) & 7, (rest >> 2) & 7)
    r_t = jnp.where(main, r & 15, 16 + (rest & 3))
    wanted = 80 * ((r_own + 4) & 7) + 40 * r_half + 20 * r_core + r_t
    ordered = dot(one_hot(iota((640, 640), 1) == wanted), o_v[...], ((1,), (0,))).astype(BF)
    o_rows[...] = ordered.reshape(2, 320, 640)

    def slab(kh):
        for kw in range(3):
            if kh == 0:
                piece = jnp.where(row == 0, zero, pltpu.roll(taps[kw], 32, 1))
            elif kh == 1:
                piece = taps[kw]
            else:
                piece = jnp.where(row == 31, zero, pltpu.roll(taps[kw], 2016, 1))
            patches[80 * kw : 80 * kw + 80, :] = piece.astype(BF)
        product = dot(patches[:, 0:1024], g_v[0:1024], ((1,), (0,)))
        if kh == 1:
            loads[4].wait()
        product = product + dot(patches[:, 1024:2048], g_v[1024:2048], ((1,), (0,)))
        t_v[0:240, :] = product.astype(BF)

    def mix(m, side, target):
        mixed = dot(o_rows[side], t_v[...], ((1,), (1,))).astype(target.dtype)
        target[m] = mixed[0:256].reshape(2, 8, 16, 256)
        for half in range(2):
            for e in range(2):
                top = 256 + 32 * half + 16 * e
                target[3, half, 3 * e + m] = mixed[top : top + 16]

    def remote(src, dst, send, recv, target):
        return pltpu.make_async_remote_copy(
            src_ref=src, dst_ref=dst, send_sem=send, recv_sem=recv, device_id=target, device_id_type=MESH
        )

    swaps = [remote(sp.at[q], db.at[q], d_send.at[q], d_recv.at[q], sibling) for q in range(4)]
    sides = {
        q: remote(
            ss.at[q, 1 - x_hi, pl.ds(0, n)], xb.at[q, pl.ds(0, n)], x_send.at[q], x_recv.at[q], partner
        )
        for q, n in enumerate((8, 8, 8, 6))
        if q not in LATE
    }
    late_sides = {
        q: remote(zb.at[i, 1 - x_hi], zx.at[i], x_send.at[q], x_recv.at[q], partner) for i, q in enumerate(LATE)
    }
    far_first = (4, 3, 5, 2, 6, 1, 7)
    scatters = [[] for q in range(4)]
    gathers = [[] for q in range(4)]
    for q in range(4):
        for j in far_first:
            peer = (z + j) % 8
            target = {"blk": blk, "dp": peer * 4 + low}
            source = ss.at[q, :, peer] if q in LATE else su.at[q, peer]
            landing = rz.at[LATE.index(q), j] if q in LATE else rb.at[q, j]
            scatters[q].append(remote(source, landing, rs_send.at[q, j], rs_recv.at[q, j], target))
            gathers[q].append(
                remote(hb.at[q, z], hb.at[q, z], ag_send.at[q, j], ag_recv.at[q, j], target)
            )
    theirs = (low + 2) % 4
    p_out = remote(pbuf.at[low], pbuf.at[low], p_send.at[0], p_recv.at[0], partner)
    p_side = remote(pbuf.at[low], pbuf.at[low], p_send.at[1], p_recv.at[1], sibling)
    p_fwd = remote(pbuf.at[theirs], pbuf.at[theirs], p_send.at[2], p_recv.at[2], sibling)
    def pair_sum(q):
        swaps[q].wait_recv()
        ss[q] = (own[q] + db[q].astype(F32)).astype(BF)
        if q in LATE:
            for copy in scatters[q]:
                copy.start()
        else:
            sides[q].start()

    loads[1].wait()
    slab(1)
    mix(0, 1 - core, sp)
    pl.semaphore_wait(barrier, 16 + jnp.where(stays, 0, 1))
    swaps[0].start()
    mix(0, core, own)
    for half in range(2):
        sp[3, half, 6:8] = jnp.zeros((2, 16, 256), BF)
        own[3, half, 6:8] = jnp.zeros((2, 16, 256), F32)
    xb[3, 6:8] = jnp.zeros((2, 16, 256), BF)
    slab(0)
    mix(1, 1 - core, sp)
    swaps[1].start()
    pair_sum(0)
    mix(1, core, own)
    slab(2)
    pair_sum(1)
    mix(2, 1 - core, sp)
    swaps[2].start()
    swaps[3].start()
    mix(2, core, own)
    pair_sum(2)
    pair_sum(3)

    loads[3].wait()
    p_out.start()
    p_side.start()

    for q in sides:
        sides[q].wait_recv()
        su[q] = (ss[q, x_hi].astype(F32) + xb[q].astype(F32)).astype(BF)
        for copy in scatters[q]:
            copy.start()

    def cross(q):
        i = LATE.index(q)
        for copy in scatters[q]:
            copy.wait_recv()
        total = ss[q, :, z].astype(F32)
        for j in range(1, 8):
            total = total + rz[i, j].astype(F32)
        zf[i] = total
        zb[i] = total.astype(BF)
        late_sides[q].start()

    def give(q):
        if q in LATE:
            late_sides[q].wait_recv()
            total = zf[LATE.index(q), x_hi] + zx[LATE.index(q)].astype(F32)
        else:
            total = su[q, z].astype(F32)
            for copy in scatters[q]:
                copy.wait_recv()
            for j in range(1, 8):
                total = total + rb[q, j].astype(F32)
        hb[q, z] = total.astype(BF)
        for copy in gathers[q]:
            copy.start()

    for act, q in STEPS:
        (cross if act == "cross" else give)(q)

    p_out.wait_recv()
    p_fwd.start()

    p_side.wait_recv()
    p_fwd.wait_recv()
    c = iota((768, 1), 0)
    part = c >> 8
    within = c & 255
    kw = (within * 52429) >> 22
    kh = jnp.where(part == 0, 1, jnp.where(part == 1, 0, 2))
    source = jnp.where(within < 240, (within - 80 * kw) * 9 + 3 * kh + kw, -1)
    order = one_hot(iota((768, 720), 1) == source)
    stacked = jnp.concatenate([dot(pbuf[s], order, ((1,), (1,))) for s in range(4)], axis=0)
    pcat[0:720, :] = stacked.astype(BF)
    pcat[720:768, :] = jnp.zeros((48, 768), BF)

    def to_plane(outgoing, incoming, send, recv, j):
        plane = (z + 12 - j) % 8
        return remote(
            outgoing.at[plane], incoming.at[blk], send.at[j], recv.at[blk], {"blk": z, "dp": plane * 4 + low}
        )

    def from_column(outgoing, incoming, send, recv, b):
        return remote(outgoing.at[b], incoming.at[b], send.at[0], recv.at[b], {"blk": b, "dp": blk * 4 + low})

    mains = [to_plane(main_out, main_in, m_send, m_recv, j) for j in range(8)]
    tails = [to_plane(tail_out, tail_in, t_send, t_recv, j) for j in range(8)]

    def send_rows(group, extra=0):
        for q in range(3):
            for copy, j in zip(gathers[q], far_first):
                if j in group:
                    copy.wait_recv()
        for i, j in enumerate(group):
            for q in range(3):
                hmat[16 * i : 16 * i + 16, 256 * q : 256 * q + 256] = hb[q, (z + 8 - j) % 8]
        n = 16 * len(group)
        product = dot(hmat[0 : n + extra, :], pcat[...], ((1,), (1,)))
        rows = product[0:n].astype(BF)
        for i, j in enumerate(group):
            main_out[(z + 12 - j) % 8] = rows[16 * i : 16 * i + 16, :]
        for j in group:
            if j == 4:
                @pl.when(jnp.logical_not(stays))
                def _():
                    mains[4].start()
            else:
                mains[j].start()
        return product[n:]

    send_rows((0, 1, 7, 2, 6))

    for copy in gathers[3]:
        copy.wait_recv()
    for m in range(3):
        for e in range(2):
            hmat[48 + 16 * e : 64 + 16 * e, 256 * m : 256 * m + 256] = hb[3, 3 * e + m]
    acc[...] = send_rows((3, 5, 4), 32)
    for k in range(8):
        tail = acc[4 * k : 4 * k + 4, :]
        pieces = [tail[:, 0:256], tail[:, 256:512], tail[:, 512:768], jnp.zeros((4, 256), F32)]
        tail_out[(k + 4) % 8] = jnp.concatenate(pieces, axis=0).astype(BF)
    for j in (0, 1, 7, 2, 6, 3, 5):
        tails[j].start()

    @pl.when(jnp.logical_not(stays))
    def _():
        tails[4].start()


    @pl.when(stays)
    def _():
        main_in[blk] = main_out[z]
        tail_in[blk] = tail_out[z]

    def collect(outgoing, incoming, send, recv):
        total = jnp.zeros(incoming.shape[1:], F32)
        for b in range(8):
            @pl.when(jnp.logical_not(jnp.logical_and(stays, blk == b)))
            def _():
                from_column(outgoing, incoming, send, recv, b).wait_recv()

            total = total + incoming[b].astype(F32)
        return total

    total = collect(main_out, main_in, m_send, m_recv)
    out_ref[0:16, :] = total[:, 0:720]
    total = collect(tail_out, tail_in, t_send, t_recv)
    out_ref[16:20, 0:256] = total[0:4, :]
    out_ref[16:20, 256:512] = total[4:8, :]
    out_ref[16:20, 512:720] = total[8:12, 0:208]

    for copy in swaps + list(sides.values()) + list(late_sides.values()) + [p_out, p_side, p_fwd] + mains[:4] + mains[5:] + tails[:4] + tails[5:]:
        copy.wait_send()
    for q in range(4):
        for copy in scatters[q] + gathers[q]:
            copy.wait_send()

    @pl.when(jnp.logical_not(stays))
    def _():
        mains[4].wait_send()
        tails[4].wait_send()


def on_device(images, out_grads, patch_inverse, output_inverse):
    dma = pltpu.SemaphoreType.DMA
    return pl.pallas_call(
        kernel,
        out_shape=jax.ShapeDtypeStruct((20, 720), F32),
        in_specs=[pl.BlockSpec(memory_space=pl.ANY)] * 4,
        out_specs=pl.BlockSpec(memory_space=pltpu.VMEM),
        scratch_shapes=[
            pltpu.VMEM((2048, 80), BF),
            pltpu.VMEM((2048, 640), BF),
            pltpu.VMEM((640, 640), BF),
            pltpu.VMEM((2, 320, 640), BF),
            pltpu.VMEM((4, 180, 720), BF),
            pltpu.VMEM((240, 2048), BF),
            pltpu.VMEM((256, 640), BF),
            pltpu.VMEM((4, 2, 8, 16, 256), F32),
            pltpu.VMEM((4, 2, 8, 16, 256), BF),
            pltpu.VMEM((4, 2, 8, 16, 256), BF),
            pltpu.VMEM((4, 2, 8, 16, 256), BF),
            pltpu.VMEM((4, 8, 16, 256), BF),
            pltpu.VMEM((4, 8, 16, 256), BF),
            pltpu.VMEM((4, 8, 16, 256), BF),
            pltpu.VMEM((len(LATE), 8, 2, 16, 256), BF),
            pltpu.VMEM((len(LATE), 2, 16, 256), F32),
            pltpu.VMEM((len(LATE), 2, 16, 256), BF),
            pltpu.VMEM((len(LATE), 16, 256), BF),
            pltpu.VMEM((4, 8, 16, 256), BF),
            pltpu.VMEM((160, 768), BF),
            pltpu.VMEM((768, 768), BF),
            pltpu.VMEM((32, 768), F32),
            pltpu.VMEM((8, 16, 768), BF),
            pltpu.VMEM((8, 16, 768), BF),
            pltpu.VMEM((8, 16, 256), BF),
            pltpu.VMEM((8, 16, 256), BF),
            dma((5,)),
            dma((3,)), dma((3,)),
            dma((4,)), dma((4,)),
            dma((4,)), dma((4,)),
            dma((4, 8)), dma((4, 8)),
            dma((4, 8)), dma((4, 8)),
            dma((8,)), dma((8,)),
            dma((8,)), dma((8,)),
        ],
        compiler_params=pltpu.CompilerParams(
            collective_id=0, has_side_effects=True, vmem_limit_bytes=60 * 1024 * 1024
        ),
        cost_estimate=pl.CostEstimate(flops=3 * 10**9, bytes_accessed=5 * 10**6, transcendentals=0),
    )(
        images.reshape(2048, 80),
        out_grads.reshape(2048, 640),
        patch_inverse.T,
        output_inverse,
    )


def solution(mesh):
    placed = (P("dp", None, None, "blk"), P("dp", None, None, None), P("blk", "dp"), P())
    return jax.shard_map(
        on_device, mesh=mesh, in_specs=placed, out_specs=P("dp", "blk"), check_vma=False
    )
```

```python
import functools

import jax
import jax.numpy as jnp
from jax import lax
from jax.experimental import pallas as pl
from jax.experimental.pallas import tpu as pltpu
from jax.sharding import PartitionSpec as P

MESH = pl.DeviceIdType.MESH
BF = jnp.bfloat16
F32 = jnp.float32
LATE = (2,)
STEPS = (('cross', 2), ('give', 0), ('give', 1), ('give', 2), ('give', 3))


def dot(a, b, dims):
    return lax.dot_general(a, b, (dims, ((), ())), preferred_element_type=F32)


def iota(shape, dim):
    return lax.broadcasted_iota(jnp.int32, shape, dim)


def one_hot(hit):
    return jnp.where(hit, 1.0, 0.0).astype(BF)


def kernel(
    img_h, g_h, p_h, o_h, out_ref,
    img_v, g_v, o_v, o_rows, pbuf, patches, t_v,
    own, sp, db, ss, xb, su, rb, rz, zf, zb, zx, hb,
    hmat, pcat, acc, main_out, main_in, tail_out, tail_in,
    load_sem, p_send, p_recv, d_send, d_recv, x_send, x_recv, rs_send, rs_recv, ag_send, ag_recv,
    m_send, m_recv, t_send, t_recv,
):
    blk = lax.axis_index("blk")
    dp = lax.axis_index("dp")
    core = dp % 2
    x_hi = (dp // 2) % 2
    z = dp // 4
    low = dp % 4
    sibling = {"blk": blk, "dp": dp + 1 - 2 * core}
    partner = {"blk": blk, "dp": dp + 2 - 4 * x_hi}
    stays = z == blk

    loads = [
        pltpu.make_async_copy(img_h, img_v, load_sem.at[0]),
        pltpu.make_async_copy(g_h.at[0:1024], g_v.at[0:1024], load_sem.at[1]),
        pltpu.make_async_copy(o_h, o_v, load_sem.at[2]),
        pltpu.make_async_copy(p_h, pbuf.at[low], load_sem.at[3]),
        pltpu.make_async_copy(g_h.at[1024:2048], g_v.at[1024:2048], load_sem.at[4]),
    ]
    for n in (0, 2, 1, 4, 3):
        loads[n].start()

    barrier = pltpu.get_barrier_semaphore()

    def greet(target):
        pl.semaphore_signal(barrier, inc=1, device_id=target, device_id_type=MESH)

    for j in range(1, 8):
        greet({"blk": (z + 8 - j) % 8, "dp": blk * 4 + low})

    @pl.when(jnp.logical_not(stays))
    def _():
        greet({"blk": z, "dp": blk * 4 + low})

    for j in range(1, 8):
        greet({"blk": blk, "dp": ((z + j) % 8) * 4 + low})
    greet(partner)
    greet(sibling)

    loads[0].wait()
    img_t = dot(one_hot(iota((80, 80), 0) == iota((80, 80), 1)), img_v[...], ((1,), (1,)))
    lane = iota((80, 2048), 1)
    col = lane & 31
    row = (lane >> 5) & 31
    zero = jnp.zeros((80, 2048), F32)
    taps = [
        jnp.where(col == 0, zero, pltpu.roll(img_t, 1, 1)),
        img_t,
        jnp.where(col == 31, zero, pltpu.roll(img_t, 2047, 1)),
    ]
    t_v[240:256, :] = jnp.zeros((16, 640), BF)

    loads[2].wait()
    r = iota((640, 1), 0)
    r_core = jnp.where(r < 320, 0, 1)
    r = r - 320 * r_core
    rest = r - 256
    main = r < 256
    r_half = jnp.where(main, r >> 7, rest >> 5)
    r_own = jnp.where(main, (r >> 4) & 7, (rest >> 2) & 7)
    r_t = jnp.where(main, r & 15, 16 + (rest & 3))
    wanted = 80 * ((r_own + 4) & 7) + 40 * r_half + 20 * r_core + r_t
    ordered = dot(one_hot(iota((640, 640), 1) == wanted), o_v[...], ((1,), (0,))).astype(BF)
    o_rows[...] = ordered.reshape(2, 320, 640)

    def slab(kh):
        for kw in range(3):
            if kh == 0:
                piece = jnp.where(row == 0, zero, pltpu.roll(taps[kw], 32, 1))
            elif kh == 1:
                piece = taps[kw]
            else:
                piece = jnp.where(row == 31, zero, pltpu.roll(taps[kw], 2016, 1))
            patches[80 * kw : 80 * kw + 80, :] = piece.astype(BF)
        product = dot(patches[:, 0:1024], g_v[0:1024], ((1,), (0,)))
        if kh == 1:
            loads[4].wait()
        product = product + dot(patches[:, 1024:2048], g_v[1024:2048], ((1,), (0,)))
        t_v[0:240, :] = product.astype(BF)

    def mix(m, side, target):
        mixed = dot(o_rows[side], t_v[...], ((1,), (1,))).astype(target.dtype)
        target[m] = mixed[0:256].reshape(2, 8, 16, 256)
        for half in range(2):
            for e in range(2):
                top = 256 + 32 * half + 16 * e
                target[3, half, 3 * e + m] = mixed[top : top + 16]

    def remote(src, dst, send, recv, target):
        return pltpu.make_async_remote_copy(
            src_ref=src, dst_ref=dst, send_sem=send, recv_sem=recv, device_id=target, device_id_type=MESH
        )

    swaps = [remote(sp.at[q], db.at[q], d_send.at[q], d_recv.at[q], sibling) for q in range(4)]
    sides = {
        q: remote(
            ss.at[q, 1 - x_hi, pl.ds(0, n)], xb.at[q, pl.ds(0, n)], x_send.at[q], x_recv.at[q], partner
        )
        for q, n in enumerate((8, 8, 8, 6))
        if q not in LATE
    }
    late_sides = {
        q: remote(zb.at[i, 1 - x_hi], zx.at[i], x_send.at[q], x_recv.at[q], partner) for i, q in enumerate(LATE)
    }
    far_first = (4, 3, 5, 2, 6, 1, 7)
    scatters = [[] for q in range(4)]
    gathers = [[] for q in range(4)]
    for q in range(4):
        for j in far_first:
            peer = (z + j) % 8
            target = {"blk": blk, "dp": peer * 4 + low}
            source = ss.at[q, :, peer] if q in LATE else su.at[q, peer]
            landing = rz.at[LATE.index(q), j] if q in LATE else rb.at[q, j]
            scatters[q].append(remote(source, landing, rs_send.at[q, j], rs_recv.at[q, j], target))
            gathers[q].append(
                remote(hb.at[q, z], hb.at[q, z], ag_send.at[q, j], ag_recv.at[q, j], target)
            )
    theirs = (low + 2) % 4
    p_out = remote(pbuf.at[low], pbuf.at[low], p_send.at[0], p_recv.at[0], partner)
    p_side = remote(pbuf.at[low], pbuf.at[low], p_send.at[1], p_recv.at[1], sibling)
    p_fwd = remote(pbuf.at[theirs], pbuf.at[theirs], p_send.at[2], p_recv.at[2], sibling)
    def pair_sum(q):
        swaps[q].wait_recv()
        ss[q] = (own[q] + db[q].astype(F32)).astype(BF)
        if q in LATE:
            for copy in scatters[q]:
                copy.start()
        else:
            sides[q].start()

    loads[1].wait()
    slab(1)
    mix(0, 1 - core, sp)
    pl.semaphore_wait(barrier, 16 + jnp.where(stays, 0, 1))
    swaps[0].start()
    mix(0, core, own)
    for half in range(2):
        sp[3, half, 6:8] = jnp.zeros((2, 16, 256), BF)
        own[3, half, 6:8] = jnp.zeros((2, 16, 256), F32)
    xb[3, 6:8] = jnp.zeros((2, 16, 256), BF)
    slab(0)
    mix(1, 1 - core, sp)
    swaps[1].start()
    pair_sum(0)
    mix(1, core, own)
    slab(2)
    pair_sum(1)
    mix(2, 1 - core, sp)
    swaps[2].start()
    swaps[3].start()
    mix(2, core, own)
    pair_sum(2)
    pair_sum(3)

    loads[3].wait()

    for q in sides:
        sides[q].wait_recv()
        if q == 1:
            p_out.start()
            p_side.start()
        su[q] = (ss[q, x_hi].astype(F32) + xb[q].astype(F32)).astype(BF)
        for copy in scatters[q]:
            copy.start()

    def cross(q):
        i = LATE.index(q)
        for copy in scatters[q]:
            copy.wait_recv()
        total = ss[q, :, z].astype(F32)
        for j in range(1, 8):
            total = total + rz[i, j].astype(F32)
        zf[i] = total
        zb[i] = total.astype(BF)
        late_sides[q].start()

    def give(q):
        if q in LATE:
            late_sides[q].wait_recv()
            total = zf[LATE.index(q), x_hi] + zx[LATE.index(q)].astype(F32)
        else:
            total = su[q, z].astype(F32)
            for copy in scatters[q]:
                copy.wait_recv()
            for j in range(1, 8):
                total = total + rb[q, j].astype(F32)
        hb[q, z] = total.astype(BF)
        for copy in gathers[q]:
            copy.start()

    for act, q in STEPS:
        (cross if act == "cross" else give)(q)

    p_out.wait_recv()
    p_fwd.start()

    p_side.wait_recv()
    p_fwd.wait_recv()
    c = iota((768, 1), 0)
    part = c >> 8
    within = c & 255
    kw = (within * 52429) >> 22
    kh = jnp.where(part == 0, 1, jnp.where(part == 1, 0, 2))
    source = jnp.where(within < 240, (within - 80 * kw) * 9 + 3 * kh + kw, -1)
    order = one_hot(iota((768, 720), 1) == source)
    stacked = jnp.concatenate([dot(pbuf[s], order, ((1,), (1,))) for s in range(4)], axis=0)
    pcat[0:720, :] = stacked.astype(BF)
    pcat[720:768, :] = jnp.zeros((48, 768), BF)

    def to_plane(outgoing, incoming, send, recv, j):
        plane = (z + 12 - j) % 8
        return remote(
            outgoing.at[plane], incoming.at[blk], send.at[j], recv.at[blk], {"blk": z, "dp": plane * 4 + low}
        )

    def from_column(outgoing, incoming, send, recv, b):
        return remote(outgoing.at[b], incoming.at[b], send.at[0], recv.at[b], {"blk": b, "dp": blk * 4 + low})

    mains = [to_plane(main_out, main_in, m_send, m_recv, j) for j in range(8)]
    tails = [to_plane(tail_out, tail_in, t_send, t_recv, j) for j in range(8)]

    def send_rows(group, extra=0):
        for q in range(3):
            for copy, j in zip(gathers[q], far_first):
                if j in group:
                    copy.wait_recv()
        for i, j in enumerate(group):
            for q in range(3):
                hmat[16 * i : 16 * i + 16, 256 * q : 256 * q + 256] = hb[q, (z + 8 - j) % 8]
        n = 16 * len(group)
        product = dot(hmat[0 : n + extra, :], pcat[...], ((1,), (1,)))
        rows = product[0:n].astype(BF)
        for i, j in enumerate(group):
            main_out[(z + 12 - j) % 8] = rows[16 * i : 16 * i + 16, :]
        for j in group:
            if j == 4:
                @pl.when(jnp.logical_not(stays))
                def _():
                    mains[4].start()
            else:
                mains[j].start()
        return product[n:]

    send_rows((0, 1, 7, 2, 6))

    for copy in gathers[3]:
        copy.wait_recv()
    for m in range(3):
        for e in range(2):
            hmat[48 + 16 * e : 64 + 16 * e, 256 * m : 256 * m + 256] = hb[3, 3 * e + m]
    acc[...] = send_rows((3, 5, 4), 32)
    for k in range(8):
        tail = acc[4 * k : 4 * k + 4, :]
        pieces = [tail[:, 0:256], tail[:, 256:512], tail[:, 512:768], jnp.zeros((4, 256), F32)]
        tail_out[(k + 4) % 8] = jnp.concatenate(pieces, axis=0).astype(BF)
    for j in (0, 1, 7, 2, 6, 3, 5):
        tails[j].start()

    @pl.when(jnp.logical_not(stays))
    def _():
        tails[4].start()


    @pl.when(stays)
    def _():
        main_in[blk] = main_out[z]
        tail_in[blk] = tail_out[z]

    def collect(outgoing, incoming, send, recv):
        total = jnp.zeros(incoming.shape[1:], F32)
        for b in range(8):
            @pl.when(jnp.logical_not(jnp.logical_and(stays, blk == b)))
            def _():
                from_column(outgoing, incoming, send, recv, b).wait_recv()

            total = total + incoming[b].astype(F32)
        return total

    total = collect(main_out, main_in, m_send, m_recv)
    out_ref[0:16, :] = total[:, 0:720]
    total = collect(tail_out, tail_in, t_send, t_recv)
    out_ref[16:20, 0:256] = total[0:4, :]
    out_ref[16:20, 256:512] = total[4:8, :]
    out_ref[16:20, 512:720] = total[8:12, 0:208]

    for copy in swaps + list(sides.values()) + list(late_sides.values()) + [p_out, p_side, p_fwd] + mains[:4] + mains[5:] + tails[:4] + tails[5:]:
        copy.wait_send()
    for q in range(4):
        for copy in scatters[q] + gathers[q]:
            copy.wait_send()

    @pl.when(jnp.logical_not(stays))
    def _():
        mains[4].wait_send()
        tails[4].wait_send()


def on_device(images, out_grads, patch_inverse, output_inverse):
    dma = pltpu.SemaphoreType.DMA
    return pl.pallas_call(
        kernel,
        out_shape=jax.ShapeDtypeStruct((20, 720), F32),
        in_specs=[pl.BlockSpec(memory_space=pl.ANY)] * 4,
        out_specs=pl.BlockSpec(memory_space=pltpu.VMEM),
        scratch_shapes=[
            pltpu.VMEM((2048, 80), BF),
            pltpu.VMEM((2048, 640), BF),
            pltpu.VMEM((640, 640), BF),
            pltpu.VMEM((2, 320, 640), BF),
            pltpu.VMEM((4, 180, 720), BF),
            pltpu.VMEM((240, 2048), BF),
            pltpu.VMEM((256, 640), BF),
            pltpu.VMEM((4, 2, 8, 16, 256), F32),
            pltpu.VMEM((4, 2, 8, 16, 256), BF),
            pltpu.VMEM((4, 2, 8, 16, 256), BF),
            pltpu.VMEM((4, 2, 8, 16, 256), BF),
            pltpu.VMEM((4, 8, 16, 256), BF),
            pltpu.VMEM((4, 8, 16, 256), BF),
            pltpu.VMEM((4, 8, 16, 256), BF),
            pltpu.VMEM((len(LATE), 8, 2, 16, 256), BF),
            pltpu.VMEM((len(LATE), 2, 16, 256), F32),
            pltpu.VMEM((len(LATE), 2, 16, 256), BF),
            pltpu.VMEM((len(LATE), 16, 256), BF),
            pltpu.VMEM((4, 8, 16, 256), BF),
            pltpu.VMEM((160, 768), BF),
            pltpu.VMEM((768, 768), BF),
            pltpu.VMEM((32, 768), F32),
            pltpu.VMEM((8, 16, 768), BF),
            pltpu.VMEM((8, 16, 768), BF),
            pltpu.VMEM((8, 16, 256), BF),
            pltpu.VMEM((8, 16, 256), BF),
            dma((5,)),
            dma((3,)), dma((3,)),
            dma((4,)), dma((4,)),
            dma((4,)), dma((4,)),
            dma((4, 8)), dma((4, 8)),
            dma((4, 8)), dma((4, 8)),
            dma((8,)), dma((8,)),
            dma((8,)), dma((8,)),
        ],
        compiler_params=pltpu.CompilerParams(
            collective_id=0, has_side_effects=True, vmem_limit_bytes=60 * 1024 * 1024
        ),
        cost_estimate=pl.CostEstimate(flops=3 * 10**9, bytes_accessed=5 * 10**6, transcendentals=0),
    )(
        images.reshape(2048, 80),
        out_grads.reshape(2048, 640),
        patch_inverse.T,
        output_inverse,
    )


def solution(mesh):
    placed = (P("dp", None, None, "blk"), P("dp", None, None, None), P("blk", "dp"), P())
    return jax.shard_map(
        on_device, mesh=mesh, in_specs=placed, out_specs=P("dp", "blk"), check_vma=False
    )
```
